512 devices in a mesh: gx: 16 (over z, x_lo), vert: 32 (over y, x_hi, core).
Axes of the slice: x: 4 (x_hi: 2, x_lo: 2; x = x_hi * 2 + x_lo), y: 8, z: 8, core: 2. Of those that a mesh axis runs over, the one named last changes fastest.
Arguments:
- dist: bfloat16 [1024, 32, 4096], P('vert', 'gx'), may hold values from 0.02 to 6
- vel_index: int32 [3, 1024], P(None, 'vert'), may hold values from 0 to 32, as said below
- weight_int: int32 [1024], P('vert'), may hold values from 1024 to 65535
Outputs:
- advanced: bfloat16 [1024, 32, 4096], P('vert', 'gx')
The draws below stay inside these ranges and needn't reach their ends.
Inputs may be any that keep to these rules, and one draw needn't show every extreme that they name: `vel_index`: in each of the three rows every node index occurs 1024 // 33 or 1024 // 33 + 1 times.
All inputs are finite; a program needn't handle non-finite values.
Results may differ from the reference program's by a relative error of at most 0.0038.
Values may be sent and summed in bfloat16 or wider, within the bound.
No kernel may reach another device: no remote copies, remote signals or barrier semaphores. Data moves between devices by JAX's collectives and lax.ppermute only.
A program may use at most 64 MiB of HBM per device.

```python
import jax
import jax.numpy as jnp
from jax import lax

NV = 1024
NODES = 33
NY = 64
NZ = 64
NX = 32
PLANE = 4096


def speed_table(key):
    balanced = jnp.arange(NV, dtype=jnp.int32) % NODES
    shuffled = [jax.random.permutation(jax.random.fold_in(key, 11 + comp), balanced) for comp in range(3)]
    return jnp.stack(shuffled).astype(jnp.int32)


def draw_vel_index(key, part):
    return speed_table(jax.random.fold_in(key, 101))


def draw_dist(key, part):
    index_table = speed_table(jax.random.fold_in(key, 101))
    nodes = 4.0 * jnp.cos(jnp.pi * jnp.arange(NODES, dtype=jnp.float32) / (NODES - 1))
    speeds = nodes[index_table]
    level_width = 1.0
    drift_width = 0.5
    group_size = min(32, NV)
    group_count = NV // group_size
    group_level = jax.random.uniform(jax.random.fold_in(key, 201), (group_count,), jnp.float32, -level_width, level_width)
    ramp = 0.4 * ((jnp.arange(NV, dtype=jnp.float32) + 0.5) * 2.0 / NV - 1.0)
    level = jnp.repeat(group_level, group_size) + ramp
    shift = jax.random.uniform(jax.random.fold_in(key, 202), (NX, PLANE), jnp.float32, -0.3, 0.3)
    drift = jax.random.uniform(jax.random.fold_in(key, 203), (3, NX, PLANE), jnp.float32, -drift_width, drift_width)
    heat = jax.random.uniform(jax.random.fold_in(key, 204), (NX, PLANE), jnp.float32, -1.0, 1.0)
    square = (speeds[0] * speeds[0] + speeds[1] * speeds[1] + speeds[2] * speeds[2]) / 48.0 - 0.5
    along = drift[0][None] * (0.25 * speeds[0])[:, None, None]
    along = along + drift[1][None] * (0.25 * speeds[1])[:, None, None]
    along = along + drift[2][None] * (0.25 * speeds[2])[:, None, None]
    rough = jnp.clip(0.3 * jax.random.normal(jax.random.fold_in(key, 205), (NV, NX, PLANE), jnp.float32), -0.9, 0.9)
    expo = level[:, None, None] + shift[None] + along + 0.8 * heat[None] * square[:, None, None] + rough
    value = jnp.clip(0.8 * jnp.exp(expo), 0.02, 6.0)
    return value.astype(jnp.bfloat16)


def place_ends(array, key, smallest, top_value):
    longest = array.shape.index(max(array.shape))
    spots = []
    for shift in (0, 1):
        where = [jax.random.randint(jax.random.fold_in(key, axis), (), 0, length) for axis, length in enumerate(array.shape)]
        where[longest] = (where[longest] + shift) % array.shape[longest]
        spots.append(tuple(where))
    return array.at[spots[0]].set(smallest).at[spots[1]].set(top_value)


def setup_inputs(seed: int = 0) -> dict:
    seeds = jax.random.split(jax.random.key(seed), 4)
    dist = draw_dist(jax.random.fold_in(seeds[3], 71), 0)
    vel_index = draw_vel_index(jax.random.fold_in(seeds[3], 71), 0)
    weight_int = place_ends(jax.random.randint(seeds[2], (NV,), 1024, 65536), jax.random.fold_in(seeds[2], 1), 1024, 65535).astype(jnp.int32)
    return dict(dist=dist, vel_index=vel_index, weight_int=weight_int)


speed_max = 4.0
time_step = 1.0 / 12.0
relax_coef = 0.1

def velocities(vel_index):
    nodes = speed_max * jnp.cos(jnp.pi * jnp.arange(NODES, dtype=jnp.float32) / (NODES - 1))
    onehot = (vel_index[:, :, None] == jnp.arange(NODES, dtype=jnp.int32)[None, None, :]).astype(jnp.float32)
    return lax.optimization_barrier(jnp.sum(onehot * nodes[None, None, :], axis=2))

def moment_rows(speeds, weight_int):
    weight = weight_int.astype(jnp.float32) * (512.0 / (32768.0 * NV))
    square = speeds[0] * speeds[0] + speeds[1] * speeds[1] + speeds[2] * speeds[2]
    return jnp.stack([weight, weight * speeds[0], weight * speeds[1], weight * speeds[2], weight * square])

def maxwell_params(moments):
    density = moments[0]
    flow = moments[1:4] / density[None]
    temper = (moments[4] / density - lax.optimization_barrier(jnp.sum(flow * flow, axis=0))) / 3.0
    scale = density * jnp.power(2.0 * jnp.pi * temper, -1.5)
    rate = time_step * relax_coef * density * jnp.sqrt(temper)
    return jnp.concatenate([flow, temper[None], scale[None], rate[None]], axis=0)

def collide(dist, speeds, params):
    grid = params.reshape(6, dist.shape[1], dist.shape[2])
    spread = jnp.zeros(dist.shape, jnp.float32)
    for comp in range(3):
        diff = speeds[comp][:, None, None] - grid[comp][None]
        spread = spread + diff * diff
    equil = grid[4][None] * jnp.exp(-spread / (2.0 * grid[3][None]))
    rate = grid[5][None]
    return ((dist.astype(jnp.float32) + rate * equil) / (1.0 + rate)).astype(jnp.bfloat16)

def stream(padded, speeds):
    values = padded.astype(jnp.float32)
    center = values[:, 1:-1]
    lower = values[:, :-2]
    upper = values[:, 2:]
    speed_x = speeds[0][:, None, None]
    flux = jnp.maximum(speed_x, 0.0) * (center - lower) + jnp.minimum(speed_x, 0.0) * (upper - center)
    count_v = center.shape[0]
    planes = center.shape[1]
    cube = center.reshape(count_v, planes, NY, NZ)
    for comp, dim in ((1, 2), (2, 3)):
        speed_k = speeds[comp][:, None, None, None]
        part = jnp.maximum(speed_k, 0.0) * (cube - jnp.roll(cube, 1, dim)) + jnp.minimum(speed_k, 0.0) * (jnp.roll(cube, -1, dim) - cube)
        flux = flux + part.reshape(count_v, planes, NY * NZ)
    return (center - time_step * flux).astype(jnp.bfloat16)

def reference(dist, vel_index, weight_int):
    speeds = velocities(vel_index)
    rows = moment_rows(speeds, weight_int)
    block = min(128, NV)
    nblock = NV // block
    dist_blocks = dist.reshape(nblock, block, NX, NY * NZ)
    row_blocks = rows.reshape(5, nblock, block).transpose(1, 0, 2)
    speed_blocks = speeds.reshape(3, nblock, block).transpose(1, 0, 2)

    def accumulate(total, item):
        part_rows, part_dist = item
        flat = part_dist.reshape(block, NX * NY * NZ).astype(jnp.float32)
        return (total + jnp.dot(part_rows, flat, precision=lax.Precision.HIGHEST), None)
    moments, _ = lax.scan(accumulate, jnp.zeros((5, NX * NY * NZ), jnp.float32), (row_blocks, dist_blocks))
    params = maxwell_params(moments)

    def advance(item):
        part_dist, part_speeds = item
        relaxed = collide(part_dist, part_speeds, params)
        padded = jnp.concatenate([relaxed[:, -1:], relaxed, relaxed[:, :1]], axis=1)
        return stream(padded, part_speeds)
    result = lax.map(advance, (dist_blocks, speed_blocks))
    return result.reshape(NV, NX, NY * NZ)
```

```python
import jax
import jax.numpy as jnp
import numpy as np
from jax import lax
from jax.experimental import pallas as pl
from jax.experimental.pallas import tpu as pltpu
from jax.sharding import Mesh, PartitionSpec as P

NV = 1024
NODES = 33
ROWS = 32
LANES = 128
CELLS = (ROWS, LANES)

speed_max = 4.0
time_step = 1.0 / 12.0
relax_coef = 0.1
center = 24.0
log2e = 1.4426950408889634

SIZES = (8, 2, 8, 2, 2)
NAMES = ("z", "xl", "y", "xh", "core")
GX = ("z", "xl")
VERT = ("y", "xh", "core")
QUAD = ("z", "xl", "xh", "core")

VMEM = pl.BlockSpec(memory_space=pltpu.VMEM)
SMEM = pl.BlockSpec(memory_space=pltpu.SMEM)


def quad_place(z, xl, xh, core):
    return ((z % SIZES[0]) * 2 + xl) * 4 + xh * 2 + core


QUADS = [
    [quad_place(z, xl, xh, 0) for xl in range(2) for xh in range(2)] for z in range(SIZES[0])
] + [
    [quad_place(z + 1 - xl, xl, xh, 1) for xl in (1, 0) for xh in range(2)]
    for z in range(SIZES[0])
]


def node_table():
    steps = np.arange(NODES, dtype=np.float64) / (NODES - 1)
    return jnp.asarray(speed_max * np.cos(np.pi * steps), jnp.float32)


def moments_kernel(index_ref, weight_ref, node_ref, low_ref, high_ref, out_ref):
    for plane, ref in enumerate((low_ref, high_ref)):
        sums = [jnp.zeros(CELLS, jnp.float32) for _ in range(5)]
        for v in range(ref.shape[0]):
            sx = node_ref[index_ref[0, v]]
            sy = node_ref[index_ref[1, v]]
            sz = node_ref[index_ref[2, v]]
            weight = weight_ref[v].astype(jnp.float32) * (512.0 / (32768.0 * NV))
            square = sx * sx + sy * sy + sz * sz
            factors = (weight, weight * sx, weight * sy, weight * sz, weight * (square - center))
            value = ref[v].astype(jnp.float32)
            sums = [total + factor * value for total, factor in zip(sums, factors)]
        for comp in range(5):
            out_ref[plane, comp] = sums[comp]


def chip_kernel(plane_ref, both_ref, out_ref):
    plane = plane_ref[0]
    for comp in range(5):
        total = (both_ref[0, plane, comp] + both_ref[1, plane, comp]).astype(out_ref.dtype)
        for copy in range(out_ref.shape[0]):
            out_ref[copy, comp] = total


def column_kernel(parts_ref, out_ref):
    for comp in range(5):
        total = parts_ref[0, comp].astype(jnp.float32)
        for part in range(1, parts_ref.shape[0]):
            total = total + parts_ref[part, comp].astype(jnp.float32)
        for copy in range(out_ref.shape[0]):
            out_ref[copy, comp] = total


def advance_kernel(
    side_ref, index_ref, node_ref, sums_ref, before_ref, low_ref, high_ref, after_ref,
    out_low_ref, out_high_ref, params_ref,
):
    side = side_ref[0]
    for plane in range(4):
        half, pair = plane // 2, 2 * (plane % 2)
        half = half + (1 - side) * (1 - 2 * half)
        total = [sums_ref[half, pair, comp] + sums_ref[half, pair + 1, comp] for comp in range(5)]
        density = total[0]
        inverse = 1.0 / density
        flow = [total[comp] * inverse for comp in (1, 2, 3)]
        speed2 = flow[0] * flow[0] + flow[1] * flow[1] + flow[2] * flow[2]
        temper = (total[4] * inverse + center - speed2) * (1.0 / 3.0)
        root = jnp.sqrt(temper)
        rate = (time_step * relax_coef) * density * root
        scale = density * ((2.0 * np.pi) ** -1.5) / (temper * root)
        keep = 1.0 / (1.0 + rate)
        for comp in range(3):
            params_ref[plane, comp] = flow[comp]
        params_ref[plane, 3] = (-0.5 * log2e) / temper
        params_ref[plane, 4] = scale * (rate * keep)
        params_ref[plane, 5] = keep

    lane = lax.broadcasted_iota(jnp.int32, CELLS, 1)

    def relax(value, plane, sx, sy, sz):
        dx = sx - params_ref[plane, 0]
        dy = sy - params_ref[plane, 1]
        dz = sz - params_ref[plane, 2]
        spread = dx * dx + dy * dy + dz * dz
        equil = params_ref[plane, 4] * jnp.exp2(spread * params_ref[plane, 3])
        mixed = value.astype(jnp.float32) * params_ref[plane, 5] + equil
        return mixed.astype(jnp.bfloat16).astype(jnp.float32)

    def step(v, carry):
        sx = node_ref[index_ref[0, v]]
        sy = node_ref[index_ref[1, v]]
        sz = node_ref[index_ref[2, v]]
        up_x, up_y, up_z = sx > 0.0, sy > 0.0, sz > 0.0
        ax, ay, az = (time_step * jnp.abs(s) for s in (sx, sy, sz))
        rest = 1.0 - (ax + ay + az)
        edge_value = jnp.where(up_x, before_ref[v].astype(jnp.float32), after_ref[v].astype(jnp.float32))
        edge = relax(edge_value, jnp.where(up_x, 0, 3), sx, sy, sz)
        low = relax(low_ref[v], 1, sx, sy, sz)
        high = relax(high_ref[v], 2, sx, sy, sz)
        from_x = (jnp.where(up_x, edge, high), jnp.where(up_x, low, edge))
        shift_z = jnp.where(up_z, 1, LANES - 1)
        wrap_z = (lane & 63) == jnp.where(up_z, 0, 63)
        wrap_y = (lane >> 6) == jnp.where(up_y, 0, 1)
        for value, beside, ref in ((low, from_x[0], out_low_ref), (high, from_x[1], out_high_ref)):
            swapped = pltpu.roll(value, 64, 1)
            row = jnp.where(up_y, pltpu.roll(swapped, 1, 0), pltpu.roll(swapped, ROWS - 1, 0))
            from_y = jnp.where(wrap_y, row, swapped)
            near = pltpu.roll(value, shift_z, 1)
            from_z = jnp.where(wrap_z, pltpu.roll(near, 64, 1), near)
            moved = rest * value + ax * beside + ay * from_y + az * from_z
            ref[v] = moved.astype(jnp.bfloat16)
        return carry

    lax.fori_loop(0, low_ref.shape[0], step, 0, unroll=2)


def shards(dist, vel_index, weight_int):
    count_v = dist.shape[0]
    nodes = node_table()
    side = lax.axis_index("xl")
    core = lax.axis_index("core")
    plane = jnp.reshape(1 ^ side ^ core, (1,)).astype(jnp.int32)
    side = jnp.reshape(side, (1,)).astype(jnp.int32)
    f32, bf16 = jnp.float32, jnp.bfloat16

    planes = dist.reshape(count_v, 2, ROWS, LANES)
    low, high = planes[:, 0], planes[:, 1]
    count = SIZES[0] * SIZES[1]
    forward = [(i, (i + 1) % count) for i in range(count)]
    backward = [(target, source) for source, target in forward]
    before = lax.ppermute(high, GX, forward)
    after = lax.ppermute(low, GX, backward)

    partial_sums = pl.pallas_call(
        moments_kernel,
        out_shape=jax.ShapeDtypeStruct((2, 5) + CELLS, f32),
        in_specs=[SMEM, SMEM, SMEM, VMEM, VMEM],
        out_specs=VMEM,
        name="moments",
    )(vel_index, weight_int, nodes, low, high)
    both = lax.all_gather(partial_sums, "core")
    chip = pl.pallas_call(
        chip_kernel,
        out_shape=jax.ShapeDtypeStruct((SIZES[2], 5) + CELLS, bf16),
        in_specs=[SMEM, VMEM],
        out_specs=VMEM,
        name="chip_sum",
    )(plane, both)
    parts = lax.all_to_all(chip, "y", 0, 0)
    column = pl.pallas_call(
        column_kernel,
        out_shape=jax.ShapeDtypeStruct((4, 5) + CELLS, f32),
        in_specs=[VMEM],
        out_specs=VMEM,
        name="column_sum",
    )(parts)
    quad = lax.all_to_all(column, QUAD, 0, 0, axis_index_groups=QUADS)
    sums = lax.all_gather(quad, "core")
    shape = jax.ShapeDtypeStruct((count_v,) + CELLS, bf16)
    out_low, out_high = pl.pallas_call(
        advance_kernel,
        out_shape=(shape, shape),
        in_specs=[SMEM, SMEM, SMEM, VMEM, VMEM, VMEM, VMEM, VMEM],
        out_specs=(VMEM, VMEM),
        scratch_shapes=[pltpu.VMEM((4, 6) + CELLS, f32)],
        name="advance",
    )(side, vel_index, nodes, sums, before, low, high, after)
    return jnp.stack([out_low, out_high], axis=1).reshape(dist.shape)


def solution(mesh):
    parts = Mesh(mesh.devices.reshape(SIZES), NAMES)
    return jax.shard_map(
        shards,
        mesh=parts,
        in_specs=(P(VERT, GX, None), P(None, VERT), P(VERT)),
        out_specs=P(VERT, GX, None),
        check_vma=False,
    )
```

```python
import jax
import jax.numpy as jnp
import numpy as np
from jax import lax
from jax.experimental import pallas as pl
from jax.experimental.pallas import tpu as pltpu
from jax.sharding import Mesh, PartitionSpec as P

NV = 1024
NODES = 33
ROWS = 32
LANES = 128
CELLS = (ROWS, LANES)
BOTH = (2 * ROWS, LANES)

speed_max = 4.0
time_step = 1.0 / 12.0
relax_coef = 0.1
center = 24.0
log2e = 1.4426950408889634

SIZES = (8, 2, 8, 2, 2)
NAMES = ("z", "xl", "y", "xh", "core")
GX = ("z", "xl")
VERT = ("y", "xh", "core")
QUAD = ("z", "xl", "xh", "core")

VMEM = pl.BlockSpec(memory_space=pltpu.VMEM)
SMEM = pl.BlockSpec(memory_space=pltpu.SMEM)
ANY = pl.BlockSpec(memory_space=pl.ANY)


def quad_place(z, xl, xh, core):
    return ((z % SIZES[0]) * 2 + xl) * 4 + xh * 2 + core


QUADS = [
    [quad_place(z, xl, xh, 0) for xl in range(2) for xh in range(2)] for z in range(SIZES[0])
] + [
    [quad_place(z + 1 - xl, xl, xh, 1) for xl in (1, 0) for xh in range(2)]
    for z in range(SIZES[0])
]


def node_table():
    steps = np.arange(NODES, dtype=np.float64) / (NODES - 1)
    return jnp.asarray(speed_max * np.cos(np.pi * steps), jnp.float32)


def small(mebibytes):
    return pltpu.CompilerParams(vmem_limit_bytes=mebibytes << 20)


def moments_kernel(index_ref, weight_ref, node_ref, dist_ref, out_ref, factor_ref, sums_ref):
    count = dist_ref.shape[0]
    for v in range(count):
        sx = node_ref[index_ref[0, v]]
        sy = node_ref[index_ref[1, v]]
        sz = node_ref[index_ref[2, v]]
        weight = weight_ref[v].astype(jnp.float32) * (512.0 / (32768.0 * NV))
        factor_ref[0, v] = weight
        factor_ref[1, v] = weight * sx
        factor_ref[2, v] = weight * sy
        factor_ref[3, v] = weight * sz
        factor_ref[4, v] = weight * (sx * sx + sy * sy + sz * sz - center)
    for part in range(2):
        rows = pl.ds(part * ROWS, ROWS)
        sums = [jnp.zeros(CELLS, jnp.float32) for _ in range(5)]
        for v in range(count):
            value = dist_ref[v, rows, :].astype(jnp.float32)
            sums = [total + factor_ref[comp, v] * value for comp, total in enumerate(sums)]
        for comp in range(5):
            sums_ref[comp, rows, :] = sums[comp]
    for plane in range(2):
        for comp in range(5):
            out_ref[plane, comp] = sums_ref[comp, pl.ds(plane, ROWS, stride=2), :]


def chip_kernel(plane_ref, both_ref, out_ref):
    plane = plane_ref[0]
    for comp in range(5):
        total = (both_ref[0, plane, comp] + both_ref[1, plane, comp]).astype(out_ref.dtype)
        for copy in range(out_ref.shape[0]):
            out_ref[copy, comp] = total


def split_kernel(after_ref, dist_ref, low_ref, high_ref, rows_ref):
    del after_ref

    def step(v, carry):
        slot = v & 3
        rows_ref[slot] = dist_ref[v].astype(jnp.float32)
        low_ref[v] = rows_ref[slot, pl.ds(0, ROWS, stride=2), :].astype(jnp.bfloat16)
        high_ref[v] = rows_ref[slot, pl.ds(1, ROWS, stride=2), :].astype(jnp.bfloat16)
        return carry

    lax.fori_loop(0, dist_ref.shape[0], step, 0, unroll=4)


def column_kernel(before_ref, after_ref, parts_ref, out_ref):
    del before_ref, after_ref
    for comp in range(5):
        total = parts_ref[0, comp].astype(jnp.float32)
        for part in range(1, parts_ref.shape[0]):
            total = total + parts_ref[part, comp].astype(jnp.float32)
        for copy in range(out_ref.shape[0]):
            out_ref[copy, comp] = total


def advance_kernel(side_ref, index_ref, node_ref, sums_ref, before_ref, dist_ref, after_ref, out_ref, own_ref, edge_params_ref, edge_ref):
    side = side_ref[0]
    for plane in range(4):
        half, pair = plane // 2, 2 * (plane % 2)
        half = half + (1 - side) * (1 - 2 * half)
        total = [sums_ref[half, pair, comp] + sums_ref[half, pair + 1, comp] for comp in range(5)]
        density = total[0]
        inverse = 1.0 / density
        flow = [total[comp] * inverse for comp in (1, 2, 3)]
        speed2 = flow[0] * flow[0] + flow[1] * flow[1] + flow[2] * flow[2]
        temper = (total[4] * inverse + center - speed2) * (1.0 / 3.0)
        root = jnp.sqrt(temper)
        rate = (time_step * relax_coef) * density * root
        scale = density * ((2.0 * np.pi) ** -1.5) / (temper * root)
        keep = 1.0 / (1.0 + rate)
        values = flow + [(-0.5 * log2e) / temper, scale * (rate * keep), keep]
        for comp in range(6):
            if plane in (1, 2):
                own_ref[comp, pl.ds(plane - 1, ROWS, stride=2), :] = values[comp]
            else:
                edge_params_ref[plane // 3, comp] = values[comp]
    lane = lax.broadcasted_iota(jnp.int32, BOTH, 1)
    parity = lax.broadcasted_iota(jnp.int32, BOTH, 0) & 1
    column = lane & 63
    upper = lane >> 6

    def relax(value, params, sx, sy, sz):
        dx = sx - params(0); dy = sy - params(1); dz = sz - params(2)
        spread = dx * dx + dy * dy + dz * dz
        equil = params(4) * jnp.exp2(spread * params(3))
        return (value.astype(jnp.float32) * params(5) + equil).astype(jnp.bfloat16).astype(jnp.float32)

    def step(v, carry):
        sx = node_ref[index_ref[0, v]]
        sy = node_ref[index_ref[1, v]]
        sz = node_ref[index_ref[2, v]]
        up_x, up_y, up_z = sx > 0.0, sy > 0.0, sz > 0.0
        ax, ay, az = (time_step * jnp.abs(s) for s in (sx, sy, sz))
        rest = 1.0 - (ax + ay + az)
        which = jnp.where(up_x, 0, 1)
        edge_value = jnp.where(up_x, before_ref[v].astype(jnp.float32), after_ref[v].astype(jnp.float32))
        edge = relax(edge_value, lambda c: edge_params_ref[which, c], sx, sy, sz)
        slot = lax.rem(v, edge_ref.shape[0])
        edge_ref[slot, pl.ds(0, ROWS, stride=2), :] = edge
        edge_ref[slot, pl.ds(1, ROWS, stride=2), :] = edge
        value = relax(dist_ref[v], lambda c: own_ref[c], sx, sy, sz)
        other = jnp.where(up_x, pltpu.roll(value, 1, 0), pltpu.roll(value, 63, 0))
        from_x = jnp.where(parity == which, edge_ref[slot], other)
        swapped = pltpu.roll(value, 64, 1)
        row = jnp.where(up_y, pltpu.roll(swapped, 2, 0), pltpu.roll(swapped, 62, 0))
        from_y = jnp.where(upper == jnp.where(up_y, 0, 1), row, swapped)
        near = pltpu.roll(value, jnp.where(up_z, 1, LANES - 1), 1)
        from_z = jnp.where(column == jnp.where(up_z, 0, 63), pltpu.roll(near, 64, 1), near)
        moved = rest * value + ax * from_x + ay * from_y + az * from_z
        out_ref[v] = moved.astype(jnp.bfloat16)
        return carry
    lax.fori_loop(0, dist_ref.shape[0], step, 0, unroll=2)


def shards(dist, vel_index, weight_int):
    count_v = dist.shape[0]
    nodes = node_table()
    side = lax.axis_index("xl")
    core = lax.axis_index("core")
    plane = jnp.reshape(1 ^ side ^ core, (1,)).astype(jnp.int32)
    side = jnp.reshape(side, (1,)).astype(jnp.int32)
    f32, bf16 = jnp.float32, jnp.bfloat16
    mixed = dist.reshape(count_v, 2, ROWS, LANES).transpose(0, 2, 1, 3).reshape((count_v,) + BOTH)

    partial_sums = pl.pallas_call(
        moments_kernel,
        out_shape=jax.ShapeDtypeStruct((2, 5) + CELLS, f32),
        in_specs=[SMEM, SMEM, SMEM, VMEM],
        out_specs=VMEM,
        scratch_shapes=[pltpu.SMEM((5, count_v), f32), pltpu.VMEM((5,) + BOTH, f32)],
        compiler_params=small(8),
        name="moments",
    )(vel_index, weight_int, nodes, mixed)
    both = lax.all_gather(partial_sums, "core")
    chip = pl.pallas_call(
        chip_kernel,
        out_shape=jax.ShapeDtypeStruct((SIZES[2], 5) + CELLS, bf16),
        in_specs=[SMEM, VMEM],
        out_specs=VMEM,
        compiler_params=small(4),
        name="chip_sum",
    )(plane, both)
    parts = lax.all_to_all(chip, "y", 0, 0)

    half = jax.ShapeDtypeStruct((count_v,) + CELLS, bf16)
    low, high = pl.pallas_call(
        split_kernel,
        out_shape=(half, half),
        in_specs=[ANY, VMEM],
        out_specs=(VMEM, VMEM),
        scratch_shapes=[pltpu.VMEM((4,) + BOTH, f32)],
        compiler_params=small(8),
        cost_estimate=pl.CostEstimate(flops=1 << 20, bytes_accessed=1 << 20, transcendentals=0),
        name="split_planes",
    )(chip, mixed)
    count = SIZES[0] * SIZES[1]
    forward = [(i, (i + 1) % count) for i in range(count)]
    backward = [(target, source) for source, target in forward]
    before = lax.ppermute(high, GX, forward)
    after = lax.ppermute(low, GX, backward)

    column = pl.pallas_call(
        column_kernel,
        out_shape=jax.ShapeDtypeStruct((4, 5) + CELLS, f32),
        in_specs=[ANY, ANY, VMEM],
        out_specs=VMEM,
        compiler_params=small(4),
        name="column_sum",
    )(before, after, parts)
    quad = lax.all_to_all(column, QUAD, 0, 0, axis_index_groups=QUADS)
    sums = lax.all_gather(quad, "core")
    out = pl.pallas_call(
        advance_kernel,
        out_shape=jax.ShapeDtypeStruct(mixed.shape, bf16),
        in_specs=[SMEM, SMEM, SMEM, VMEM, VMEM, VMEM, VMEM],
        out_specs=VMEM,
        scratch_shapes=[
            pltpu.VMEM((6,) + BOTH, f32),
            pltpu.VMEM((2, 6) + CELLS, f32),
            pltpu.VMEM((4,) + BOTH, f32),
        ],
        compiler_params=small(16),
        name="advance",
    )(side, vel_index, nodes, sums, before, mixed, after)
    return out.reshape(count_v, ROWS, 2, LANES).transpose(0, 2, 1, 3).reshape(dist.shape)


def solution(mesh):
    parts = Mesh(mesh.devices.reshape(SIZES), NAMES)
    return jax.shard_map(
        shards,
        mesh=parts,
        in_specs=(P(VERT, GX, None), P(None, VERT), P(VERT)),
        out_specs=P(VERT, GX, None),
        check_vma=False,
    )
```

```python
import jax
import jax.numpy as jnp
import numpy as np
from jax import lax
from jax.experimental import pallas as pl
from jax.experimental.pallas import tpu as pltpu
from jax.sharding import Mesh, PartitionSpec as P

NV = 1024
NODES = 33
ROWS = 32
LANES = 128
CELLS = (ROWS, LANES)
BOTH = (2 * ROWS, LANES)

speed_max = 4.0
time_step = 1.0 / 12.0
relax_coef = 0.1
center = 24.0
log2e = 1.4426950408889634

SIZES = (8, 2, 8, 2, 2)
NAMES = ("z", "xl", "y", "xh", "core")
GX = ("z", "xl")
VERT = ("y", "xh", "core")

VMEM = pl.BlockSpec(memory_space=pltpu.VMEM)
SMEM = pl.BlockSpec(memory_space=pltpu.SMEM)
ANY = pl.BlockSpec(memory_space=pl.ANY)
HBM = pl.BlockSpec(memory_space=pltpu.HBM)


OWNERS = SIZES[2] * SIZES[3]
SHARE = ROWS // OWNERS
CHUNK = 16


def place(z, xl, y, xh, core):
    return ((((z % SIZES[0]) * 2 + xl) * SIZES[2] + y) * 2 + xh) * 2 + core


PAIRS = [[(z, 0, 0), (z, 1, 0)] for z in range(SIZES[0])] + [
    [(z, 1, 1), (z + 1, 0, 1)] for z in range(SIZES[0])
]
GROUPS = [
    [place(z, xl, y, xh, core) for z, xl, core in pair for y in range(SIZES[2]) for xh in range(2)]
    for pair in PAIRS
]
NODE_SPEEDS = [float(speed_max * np.cos(np.pi * j / (NODES - 1))) for j in range(NODES)]


def fill_nodes(node_ref):
    for j, speed in enumerate(NODE_SPEEDS):
        node_ref[j] = jnp.float32(speed)


def small(mebibytes):
    return pltpu.CompilerParams(vmem_limit_bytes=mebibytes << 20)


def moments_kernel(
    side_ref, index_hbm, weight_hbm, dist_hbm, out_ref,
    index_ref, weight_ref, node_ref, factor_ref, dist_ref, sums_ref, chunk_ref, small_sems, sems,
):
    count = dist_ref.shape[0]
    half = count // 2
    pieces = []
    for part in range(2):
        for k in range(2):
            where = (pl.ds(k * half, half), pl.ds(part * ROWS, ROWS))
            pieces.append(pltpu.make_async_copy(dist_hbm.at[where], dist_ref.at[where], sems.at[2 * part + k]))
    tables = [
        pltpu.make_async_copy(index_hbm, index_ref, small_sems.at[0]),
        pltpu.make_async_copy(weight_hbm, weight_ref, small_sems.at[1]),
    ]
    for copy in tables + pieces:
        copy.start()
    fill_nodes(node_ref)
    for copy in tables:
        copy.wait()
    for v in range(count):
        sx = node_ref[index_ref[0, v]]
        sy = node_ref[index_ref[1, v]]
        sz = node_ref[index_ref[2, v]]
        weight = weight_ref[v].astype(jnp.float32) * (512.0 / (32768.0 * NV))
        factor_ref[0, v] = weight
        factor_ref[1, v] = weight * sx
        factor_ref[2, v] = weight * sy
        factor_ref[3, v] = weight * sz
        factor_ref[4, v] = weight * (sx * sx + sy * sy + sz * sz - center)
    for part in range(2):
        rows = pl.ds(part * ROWS, ROWS)
        sums = [jnp.zeros(CELLS, jnp.float32) for _ in range(5)]
        for v in range(count):
            if v % half == 0:
                pieces[2 * part + v // half].wait()
            value = dist_ref[v, rows, :].astype(jnp.float32)
            sums = [total + factor_ref[comp, v] * value for comp, total in enumerate(sums)]
        for comp in range(5):
            sums_ref[comp, rows, :] = sums[comp]
    side = side_ref[0]
    for core in range(2):
        plane = 1 - core + side * (2 * core - 1)
        for comp in range(5):
            for r in range(SHARE):
                picked = sums_ref[comp, pl.ds(SHARE * r + plane, OWNERS, stride=2 * SHARE), :]
                chunk_ref[core, pl.ds(SHARE * comp + r, OWNERS, stride=CHUNK), :] = picked
        for r in range(5 * SHARE, CHUNK):
            chunk_ref[core, pl.ds(r, OWNERS, stride=CHUNK), :] = jnp.zeros((OWNERS, LANES), jnp.float32)
        for e in range(OWNERS):
            out_ref[2 * e + core] = chunk_ref[core, pl.ds(CHUNK * e, CHUNK), :].astype(out_ref.dtype)


def split_kernel(token_ref, dist_ref, low_ref, high_a_ref, high_b_ref, rows_ref):
    del token_ref
    half = high_a_ref.shape[0]

    def step(v, carry):
        for k, high_ref in enumerate((high_a_ref, high_b_ref)):
            slot, at = 2 * (v & 1) + k, v + k * half
            rows_ref[slot] = dist_ref[at].astype(jnp.float32)
            low_ref[at] = rows_ref[slot, pl.ds(0, ROWS, stride=2), :].astype(jnp.bfloat16)
            high_ref[v] = rows_ref[slot, pl.ds(1, ROWS, stride=2), :].astype(jnp.bfloat16)
        return carry

    lax.fori_loop(0, half, step, 0, unroll=2)


def owner_kernel(token_a_ref, token_b_ref, parts_ref, out_ref):
    del token_a_ref, token_b_ref
    total = parts_ref[0].astype(jnp.float32)
    for part in range(1, parts_ref.shape[0]):
        total = total + parts_ref[part].astype(jnp.float32)
    for copy in range(out_ref.shape[0]):
        out_ref[copy] = total


def advance_kernel(
    side_ref, index_ref, sums_ref, before_ref, dist_ref, after_ref, out_ref,
    node_ref, own_ref, edge_params_ref, edge_ref,
):
    fill_nodes(node_ref)
    side = side_ref[0]
    for plane, r in [(plane, r) for plane in range(4) for r in range(SHARE)]:
        half, pair = plane // 2, plane % 2
        half = half + (1 - side) * (1 - 2 * half)
        first = pair * OWNERS * CHUNK + r
        total = [
            sums_ref[half, pl.ds(first + SHARE * comp, OWNERS, stride=CHUNK), :] for comp in range(5)
        ]
        density = total[0]
        inverse = 1.0 / density
        flow = [total[comp] * inverse for comp in (1, 2, 3)]
        speed2 = flow[0] * flow[0] + flow[1] * flow[1] + flow[2] * flow[2]
        temper = (total[4] * inverse + center - speed2) * (1.0 / 3.0)
        root = jnp.sqrt(temper)
        rate = (time_step * relax_coef) * density * root
        scale = density * ((2.0 * np.pi) ** -1.5) / (temper * root)
        keep = 1.0 / (1.0 + rate)
        values = flow + [(-0.5 * log2e) / temper, scale * (rate * keep), keep]
        for comp in range(6):
            if plane in (1, 2):
                rows = pl.ds(2 * r + plane - 1, OWNERS, stride=2 * SHARE)
                own_ref[comp, rows, :] = values[comp]
            else:
                edge_params_ref[plane // 3, comp, pl.ds(r, OWNERS, stride=SHARE), :] = values[comp]
    lane = lax.broadcasted_iota(jnp.int32, BOTH, 1)
    parity = lax.broadcasted_iota(jnp.int32, BOTH, 0) & 1
    column = lane & 63
    upper = lane >> 6

    def relax(value, params, sx, sy, sz):
        dx = sx - params(0); dy = sy - params(1); dz = sz - params(2)
        spread = dx * dx + dy * dy + dz * dz
        equil = params(4) * jnp.exp2(spread * params(3))
        return (value.astype(jnp.float32) * params(5) + equil).astype(jnp.bfloat16).astype(jnp.float32)

    def step(v, carry):
        sx = node_ref[index_ref[0, v]]
        sy = node_ref[index_ref[1, v]]
        sz = node_ref[index_ref[2, v]]
        up_x, up_y, up_z = sx > 0.0, sy > 0.0, sz > 0.0
        ax, ay, az = (time_step * jnp.abs(s) for s in (sx, sy, sz))
        rest = 1.0 - (ax + ay + az)
        which = jnp.where(up_x, 0, 1)
        edge_value = jnp.where(up_x, before_ref[v].astype(jnp.float32), after_ref[v].astype(jnp.float32))
        edge = relax(edge_value, lambda c: edge_params_ref[which, c], sx, sy, sz)
        slot = lax.rem(v, edge_ref.shape[0])
        edge_ref[slot, pl.ds(0, ROWS, stride=2), :] = edge
        edge_ref[slot, pl.ds(1, ROWS, stride=2), :] = edge
        value = relax(dist_ref[v], lambda c: own_ref[c], sx, sy, sz)
        other = jnp.where(up_x, pltpu.roll(value, 1, 0), pltpu.roll(value, 63, 0))
        from_x = jnp.where(parity == which, edge_ref[slot], other)
        swapped = pltpu.roll(value, 64, 1)
        row = jnp.where(up_y, pltpu.roll(swapped, 2, 0), pltpu.roll(swapped, 62, 0))
        from_y = jnp.where(upper == jnp.where(up_y, 0, 1), row, swapped)
        near = pltpu.roll(value, jnp.where(up_z, 1, LANES - 1), 1)
        from_z = jnp.where(column == jnp.where(up_z, 0, 63), pltpu.roll(near, 64, 1), near)
        moved = rest * value + ax * from_x + ay * from_y + az * from_z
        out_ref[v] = moved.astype(jnp.bfloat16)
        return carry
    lax.fori_loop(0, dist_ref.shape[0], step, 0, unroll=2)


def shards(dist, vel_index, weight_int):
    count_v = dist.shape[0]
    side = jnp.reshape(lax.axis_index("xl"), (1,)).astype(jnp.int32)
    f32, bf16 = jnp.float32, jnp.bfloat16
    mixed = dist.reshape(count_v, 2, ROWS, LANES).transpose(0, 2, 1, 3).reshape((count_v,) + BOTH)

    chunks = pl.pallas_call(
        moments_kernel,
        out_shape=jax.ShapeDtypeStruct((2 * OWNERS, CHUNK, LANES), bf16),
        in_specs=[SMEM, HBM, HBM, HBM],
        out_specs=VMEM,
        scratch_shapes=[
            pltpu.SMEM(vel_index.shape, jnp.int32),
            pltpu.SMEM(weight_int.shape, jnp.int32),
            pltpu.SMEM((NODES,), f32),
            pltpu.SMEM((5, count_v), f32),
            pltpu.VMEM(mixed.shape, bf16),
            pltpu.VMEM((5,) + BOTH, f32),
            pltpu.VMEM((2, OWNERS * CHUNK, LANES), f32),
            pltpu.SemaphoreType.DMA((2,)),
            pltpu.SemaphoreType.DMA((4,)),
        ],
        compiler_params=small(56),
        name="moments",
    )(side, vel_index, weight_int, mixed)
    parts = lax.all_to_all(chunks, VERT, 0, 0)

    whole = jax.ShapeDtypeStruct((count_v,) + CELLS, bf16)
    half = jax.ShapeDtypeStruct((count_v // 2,) + CELLS, bf16)
    low, high_a, high_b = pl.pallas_call(
        split_kernel,
        out_shape=(whole, half, half),
        in_specs=[ANY, VMEM],
        out_specs=(VMEM, VMEM, VMEM),
        scratch_shapes=[pltpu.VMEM((4,) + BOTH, f32)],
        compiler_params=small(8),
        cost_estimate=pl.CostEstimate(flops=1 << 33, bytes_accessed=1 << 25, transcendentals=0),
        name="split_planes",
    )(chunks, mixed)
    count = SIZES[0] * SIZES[1]
    forward = [(i, (i + 1) % count) for i in range(count)]
    backward = [(target, source) for source, target in forward]
    before_a = lax.ppermute(high_a, GX, forward)
    before_b = lax.ppermute(high_b, GX, forward)
    after = lax.ppermute(low, GX, backward)

    owned = pl.pallas_call(
        owner_kernel,
        out_shape=jax.ShapeDtypeStruct((2 * OWNERS, CHUNK, LANES), f32),
        in_specs=[ANY, ANY, VMEM],
        out_specs=VMEM,
        compiler_params=small(4),
        name="owner_sum",
    )(before_a, before_b, parts)
    before = jnp.concatenate([before_a, before_b])
    gathered = lax.all_to_all(owned, NAMES, 0, 0, axis_index_groups=GROUPS)
    sums = lax.all_gather(gathered.reshape(2 * OWNERS * CHUNK, LANES), "core")
    out = pl.pallas_call(
        advance_kernel,
        out_shape=jax.ShapeDtypeStruct(mixed.shape, bf16),
        in_specs=[SMEM, SMEM, VMEM, VMEM, VMEM, VMEM],
        out_specs=VMEM,
        scratch_shapes=[
            pltpu.SMEM((NODES,), f32),
            pltpu.VMEM((6,) + BOTH, f32),
            pltpu.VMEM((2, 6) + CELLS, f32),
            pltpu.VMEM((4,) + BOTH, f32),
        ],
        compiler_params=small(16),
        name="advance",
    )(side, vel_index, sums, before, mixed, after)
    return out.reshape(count_v, ROWS, 2, LANES).transpose(0, 2, 1, 3).reshape(dist.shape)


def solution(mesh):
    parts = Mesh(mesh.devices.reshape(SIZES), NAMES)
    return jax.shard_map(
        shards,
        mesh=parts,
        in_specs=(P(VERT, GX, None), P(None, VERT), P(VERT)),
        out_specs=P(VERT, GX, None),
        check_vma=False,
    )
```

```python
import jax
import jax.numpy as jnp
import numpy as np
from jax import lax
from jax.experimental import pallas as pl
from jax.experimental.pallas import tpu as pltpu
from jax.sharding import Mesh, PartitionSpec as P

NV = 1024
NODES = 33
ROWS = 32
LANES = 128
CELLS = (ROWS, LANES)
BOTH = (2 * ROWS, LANES)

speed_max = 4.0
time_step = 1.0 / 12.0
relax_coef = 0.1
center = 24.0
log2e = 1.4426950408889634

SIZES = (8, 2, 8, 2, 2)
NAMES = ("z", "xl", "y", "xh", "core")
GX = ("z", "xl")
VERT = ("y", "xh", "core")

VMEM = pl.BlockSpec(memory_space=pltpu.VMEM)
HBM = pl.BlockSpec(memory_space=pltpu.HBM)
SMEM = pl.BlockSpec(memory_space=pltpu.SMEM)


HALF = ROWS // 2


def place(z, xl, y, xh, core):
    return ((((z % SIZES[0]) * 2 + xl) * SIZES[2] + y) * 2 + xh) * 2 + core


PAIRS = [[(z, 0, 0), (z, 1, 0)] for z in range(SIZES[0])] + [
    [(z, 1, 1), (z + 1, 0, 1)] for z in range(SIZES[0])
]
GROUPS = [
    [place(z, xl, y + odd, xh, core) for z, xl, core in pair for odd in range(2) for xh in range(2)]
    for pair in PAIRS
    for y in range(0, SIZES[2], 2)
]
NODE_SPEEDS = [float(speed_max * np.cos(np.pi * j / (NODES - 1))) for j in range(NODES)]


def fill_nodes(node_ref):
    for j, speed in enumerate(NODE_SPEEDS):
        node_ref[j] = jnp.float32(speed)


def small(mebibytes):
    return pltpu.CompilerParams(vmem_limit_bytes=mebibytes << 20)


def moments_kernel(
    index_hbm, weight_hbm, dist_hbm, out_ref,
    index_ref, weight_ref, node_ref, factor_ref, dist_ref, sums_ref, table_sems, sems,
):
    count = dist_ref.shape[0]
    half = count // 2
    pieces = []
    for part in range(2):
        for k in range(2):
            where = (pl.ds(k * half, half), pl.ds(part * ROWS, ROWS))
            pieces.append(pltpu.make_async_copy(dist_hbm.at[where], dist_ref.at[where], sems.at[2 * part + k]))
    tables = [
        pltpu.make_async_copy(index_hbm, index_ref, table_sems.at[0]),
        pltpu.make_async_copy(weight_hbm, weight_ref, table_sems.at[1]),
    ]
    for copy in tables + pieces:
        copy.start()
    fill_nodes(node_ref)
    for copy in tables:
        copy.wait()
    for v in range(count):
        sx = node_ref[index_ref[0, v]]
        sy = node_ref[index_ref[1, v]]
        sz = node_ref[index_ref[2, v]]
        weight = weight_ref[v].astype(jnp.float32) * (512.0 / (32768.0 * NV))
        factor_ref[0, v] = weight
        factor_ref[1, v] = weight * sx
        factor_ref[2, v] = weight * sy
        factor_ref[3, v] = weight * sz
        factor_ref[4, v] = weight * (sx * sx + sy * sy + sz * sz - center)
    for part in range(2):
        rows = pl.ds(part * ROWS, ROWS)
        sums = [jnp.zeros(CELLS, jnp.float32) for _ in range(5)]
        for v in range(count):
            if v % half == 0:
                pieces[2 * part + v // half].wait()
            value = dist_ref[v, rows, :].astype(jnp.float32)
            sums = [total + factor_ref[comp, v] * value for comp, total in enumerate(sums)]
        for comp in range(5):
            sums_ref[comp, rows, :] = sums[comp]
    for plane in range(2):
        for comp in range(5):
            out_ref[plane, comp] = sums_ref[comp, pl.ds(plane, ROWS, stride=2), :]


def chip_kernel(plane_ref, both_ref, out_ref):
    plane = plane_ref[0]
    for comp in range(5):
        total = (both_ref[0, plane, comp] + both_ref[1, plane, comp]).astype(out_ref.dtype)
        for y in range(out_ref.shape[0]):
            first = HALF * (y % 2)
            out_ref[y, comp] = total[first:first + HALF]


def split_kernel(side_ref, dist_ref, within_ref, passed_ref, rows_ref):
    side = side_ref[0]

    def step(v, carry):
        slot = v & 3
        rows_ref[slot] = dist_ref[v].astype(jnp.float32)
        within_ref[v] = rows_ref[slot, pl.ds(side, ROWS, stride=2), :].astype(jnp.bfloat16)
        passed_ref[v] = rows_ref[slot, pl.ds(1 - side, ROWS, stride=2), :].astype(jnp.bfloat16)
        return carry

    lax.fori_loop(0, dist_ref.shape[0], step, 0, unroll=4)


def column_kernel(parts_ref, out_ref):
    for comp in range(5):
        total = parts_ref[0, comp].astype(jnp.float32)
        for part in range(1, parts_ref.shape[0]):
            total = total + parts_ref[part, comp].astype(jnp.float32)
        for copy in range(out_ref.shape[0]):
            out_ref[copy, comp] = total


def advance_kernel(
    side_ref, index_ref, sums_ref, across_ref, dist_ref, within_ref, out_ref,
    node_ref, own_ref, edge_params_ref, edge_ref,
):
    side = side_ref[0]
    fill_nodes(node_ref)
    for plane, part in [(plane, part) for plane in range(4) for part in range(2)]:
        core, first = plane // 2, 4 * (plane % 2) + 2 * part
        core = core + (1 - side) * (1 - 2 * core)
        total = [sums_ref[core, first, comp] + sums_ref[core, first + 1, comp] for comp in range(5)]
        density = total[0]
        inverse = 1.0 / density
        flow = [total[comp] * inverse for comp in (1, 2, 3)]
        speed2 = flow[0] * flow[0] + flow[1] * flow[1] + flow[2] * flow[2]
        temper = (total[4] * inverse + center - speed2) * (1.0 / 3.0)
        root = jnp.sqrt(temper)
        rate = (time_step * relax_coef) * density * root
        scale = density * ((2.0 * np.pi) ** -1.5) / (temper * root)
        keep = 1.0 / (1.0 + rate)
        values = flow + [(-0.5 * log2e) / temper, scale * (rate * keep), keep]
        for comp in range(6):
            if plane in (1, 2):
                own_ref[comp, pl.ds(2 * HALF * part + plane - 1, HALF, stride=2), :] = values[comp]
            else:
                edge_params_ref[plane // 3, comp, pl.ds(HALF * part, HALF), :] = values[comp]
    lane8 = lax.broadcasted_iota(jnp.int32, (8,128), 1)
    sub8 = lax.broadcasted_iota(jnp.int32, (8,128), 0)
    column = lane8 & 63; upper = lane8 >> 6; parity = sub8 & 1

    def relax(value, params, sx, sy, sz):
        dx = sx - params(0); dy = sy - params(1); dz = sz - params(2)
        spread = dx * dx + dy * dy + dz * dz
        equil = params(4) * jnp.exp2(spread * params(3))
        return (value.astype(jnp.float32) * params(5) + equil).astype(jnp.bfloat16).astype(jnp.float32)

    def step(v, carry):
        sx = node_ref[index_ref[0, v]]
        sy = node_ref[index_ref[1, v]]
        sz = node_ref[index_ref[2, v]]
        up_x, up_y, up_z = sx > 0.0, sy > 0.0, sz > 0.0
        ax, ay, az = (time_step * jnp.abs(s) for s in (sx, sy, sz))
        rest = 1.0 - (ax + ay + az)
        which = jnp.where(up_x, 0, 1)
        edge_value = jnp.where(which == side, across_ref[v].astype(jnp.float32), within_ref[v].astype(jnp.float32))
        edge = relax(edge_value, lambda c: edge_params_ref[which, c], sx, sy, sz)
        slot = lax.rem(v, edge_ref.shape[0])
        edge_ref[slot, pl.ds(0, ROWS, stride=2), :] = edge
        edge_ref[slot, pl.ds(1, ROWS, stride=2), :] = edge
        xmask = parity == which
        s1 = jnp.where(up_x, 1, 7); s2 = jnp.where(up_y, 2, 6)
        xlast = sub8 == jnp.where(up_x, 0, 7)
        ylast = (sub8 >> 1) == jnp.where(up_y, 0, 3)
        ymask = upper == jnp.where(up_y, 0, 1)
        zmask = column == jnp.where(up_z, 0, 63)
        shift_z = jnp.where(up_z, 1, LANES - 1)
        raw = dist_ref[v].astype(jnp.float32)
        vals=[relax(raw[8*k:8*k+8], lambda c, k=k: own_ref[c, 8*k:8*k+8, :], sx, sy, sz) for k in range(8)]
        sw=[pltpu.roll(a,64,1) for a in vals]
        ry=[pltpu.roll(a,s2,0) for a in sw]
        rx=[pltpu.roll(a,s1,0) for a in vals]
        outs=[]
        for k in range(8):
            e = edge_ref[slot, 8*k:8*k+8, :]
            from_x = jnp.where(xmask, e, rx[k])
            nb = jnp.where(up_y, ry[(k-1)%8], ry[(k+1)%8])
            row = jnp.where(ylast, nb, ry[k])
            from_y = jnp.where(ymask, row, sw[k])
            near = pltpu.roll(vals[k], shift_z, 1)
            from_z = jnp.where(zmask, pltpu.roll(near, 64, 1), near)
            outs.append(rest*vals[k]+ax*from_x+ay*from_y+az*from_z)
        out_ref[v] = jnp.concatenate(outs,0).astype(jnp.bfloat16)
        return carry
    lax.fori_loop(0, dist_ref.shape[0], step, 0, unroll=8)


def shards(dist, vel_index, weight_int):
    count_v = dist.shape[0]
    side = lax.axis_index("xl")
    core = lax.axis_index("core")
    plane = jnp.reshape(1 ^ side ^ core, (1,)).astype(jnp.int32)
    side = jnp.reshape(side, (1,)).astype(jnp.int32)
    f32, bf16 = jnp.float32, jnp.bfloat16
    mixed = dist.reshape(count_v, 2, ROWS, LANES).transpose(0, 2, 1, 3).reshape((count_v,) + BOTH)

    partial_sums = pl.pallas_call(
        moments_kernel,
        out_shape=jax.ShapeDtypeStruct((2, 5) + CELLS, f32),
        in_specs=[HBM, HBM, HBM],
        out_specs=VMEM,
        scratch_shapes=[
            pltpu.SMEM(vel_index.shape, jnp.int32),
            pltpu.SMEM(weight_int.shape, jnp.int32),
            pltpu.SMEM((NODES,), f32),
            pltpu.SMEM((5, count_v), f32),
            pltpu.VMEM(mixed.shape, bf16),
            pltpu.VMEM((5,) + BOTH, f32),
            pltpu.SemaphoreType.DMA((2,)),
            pltpu.SemaphoreType.DMA((4,)),
        ],
        compiler_params=small(56),
        name="moments",
    )(vel_index, weight_int, mixed)
    both = lax.all_gather(partial_sums, "core")
    chip = pl.pallas_call(
        chip_kernel,
        out_shape=jax.ShapeDtypeStruct((SIZES[2], 5, HALF, LANES), bf16),
        in_specs=[SMEM, VMEM],
        out_specs=VMEM,
        compiler_params=small(4),
        name="chip_sum",
    )(plane, both)
    parts = lax.all_to_all(chip, "y", 0, 0)

    count = SIZES[0] * SIZES[1]
    beside = lax.ppermute(mixed, GX, [(i, i ^ 1) for i in range(count)])
    half = jax.ShapeDtypeStruct((count_v,) + CELLS, bf16)
    within, passed = pl.pallas_call(
        split_kernel,
        out_shape=(half, half),
        in_specs=[SMEM, VMEM],
        out_specs=(VMEM, VMEM),
        scratch_shapes=[pltpu.VMEM((4,) + BOTH, f32)],
        compiler_params=small(8),
        cost_estimate=pl.CostEstimate(flops=1 << 20, bytes_accessed=1 << 20, transcendentals=0),
        name="split_planes",
    )(side, beside)
    across = lax.ppermute(passed, GX, [(i, (i + 2 - 4 * (i % 2)) % count) for i in range(count)])

    column = pl.pallas_call(
        column_kernel,
        out_shape=jax.ShapeDtypeStruct((8, 5, HALF, LANES), f32),
        in_specs=[VMEM],
        out_specs=VMEM,
        compiler_params=small(4),
        name="column_sum",
    )(parts)
    gathered = lax.all_to_all(column, NAMES, 0, 0, axis_index_groups=GROUPS)
    sums = lax.all_gather(gathered, "core")
    out = pl.pallas_call(
        advance_kernel,
        out_shape=jax.ShapeDtypeStruct(mixed.shape, bf16),
        in_specs=[SMEM, SMEM, VMEM, VMEM, VMEM, VMEM],
        out_specs=VMEM,
        scratch_shapes=[
            pltpu.SMEM((NODES,), f32),
            pltpu.VMEM((6,) + BOTH, f32),
            pltpu.VMEM((2, 6) + CELLS, f32),
            pltpu.VMEM((8,) + BOTH, f32),
        ],
        compiler_params=small(16),
        name="advance",
    )(side, vel_index, sums, across, mixed, within)
    return out.reshape(count_v, ROWS, 2, LANES).transpose(0, 2, 1, 3).reshape(dist.shape)


def solution(mesh):
    parts = Mesh(mesh.devices.reshape(SIZES), NAMES)
    return jax.shard_map(
        shards,
        mesh=parts,
        in_specs=(P(VERT, GX, None), P(None, VERT), P(VERT)),
        out_specs=P(VERT, GX, None),
        check_vma=False,
    )
```

```python
import jax
import jax.numpy as jnp
import numpy as np
from jax import lax
from jax.experimental import pallas as pl
from jax.experimental.pallas import tpu as pltpu
from jax.sharding import Mesh, PartitionSpec as P

NV = 1024
NODES = 33
ROWS = 32
LANES = 128
CELLS = (ROWS, LANES)
BOTH = (2 * ROWS, LANES)

speed_max = 4.0
time_step = 1.0 / 12.0
relax_coef = 0.1
center = 24.0
log2e = 1.4426950408889634

SIZES = (8, 2, 8, 2, 2)
NAMES = ("z", "xl", "y", "xh", "core")
GX = ("z", "xl")
VERT = ("y", "xh", "core")

VMEM = pl.BlockSpec(memory_space=pltpu.VMEM)
HBM = pl.BlockSpec(memory_space=pltpu.HBM)
SMEM = pl.BlockSpec(memory_space=pltpu.SMEM)


HALF = ROWS // 2


def place(z, xl, y, xh, core):
    return ((((z % SIZES[0]) * 2 + xl) * SIZES[2] + y) * 2 + xh) * 2 + core


PAIRS = [[(z, 0, 0), (z, 1, 0)] for z in range(SIZES[0])] + [
    [(z, 1, 1), (z + 1, 0, 1)] for z in range(SIZES[0])
]
GROUPS = [
    [place(z, xl, y + odd, xh, core) for z, xl, core in pair for odd in range(2) for xh in range(2)]
    for pair in PAIRS
    for y in range(0, SIZES[2], 2)
]
NODE_SPEEDS = [float(speed_max * np.cos(np.pi * j / (NODES - 1))) for j in range(NODES)]


def fill_nodes(node_ref):
    for j, speed in enumerate(NODE_SPEEDS):
        node_ref[j] = jnp.float32(speed)


def scalars(index_ref, node_ref, v):
    return [node_ref[index_ref[comp, v]] for comp in range(3)]


def small(mebibytes):
    return pltpu.CompilerParams(vmem_limit_bytes=mebibytes << 20)


def moments_kernel(
    index_hbm, weight_hbm, dist_hbm, out_ref,
    index_ref, weight_ref, node_ref, dist_ref, sums_ref, table_sems, sems,
):
    count = dist_ref.shape[0]
    half = count // 2
    pieces = []
    for part in range(2):
        for k in range(2):
            where = (pl.ds(k * half, half), pl.ds(part * ROWS, ROWS))
            pieces.append(pltpu.make_async_copy(dist_hbm.at[where], dist_ref.at[where], sems.at[2 * part + k]))
    tables = [
        pltpu.make_async_copy(index_hbm, index_ref, table_sems.at[0]),
        pltpu.make_async_copy(weight_hbm, weight_ref, table_sems.at[1]),
    ]
    for copy in tables + pieces:
        copy.start()
    fill_nodes(node_ref)
    for copy in tables:
        copy.wait()
    for part in range(2):
        rows = pl.ds(part * ROWS, ROWS)
        sums = [jnp.zeros(CELLS, jnp.float32) for _ in range(5)]
        for v in range(count):
            if v % half == 0:
                pieces[2 * part + v // half].wait()
            sx, sy, sz = scalars(index_ref, node_ref, v)
            weight = weight_ref[v].astype(jnp.float32) * (512.0 / (32768.0 * NV))
            square = sx * sx + sy * sy + sz * sz - center
            value = weight * dist_ref[v, rows, :].astype(jnp.float32)
            terms = (value, sx * value, sy * value, sz * value, square * value)
            sums = [total + term for total, term in zip(sums, terms)]
        for comp in range(5):
            sums_ref[comp, rows, :] = sums[comp]
    for plane in range(2):
        for comp in range(5):
            out_ref[plane, comp] = sums_ref[comp, pl.ds(plane, ROWS, stride=2), :]


def chip_kernel(plane_ref, both_ref, out_ref):
    plane = plane_ref[0]
    for comp in range(5):
        total = (both_ref[0, plane, comp] + both_ref[1, plane, comp]).astype(out_ref.dtype)
        for y in range(out_ref.shape[0]):
            first = HALF * (y % 2)
            out_ref[y, comp] = total[first:first + HALF]


def copy_kernel(in_ref, out_ref):
    out_ref[...] = in_ref[...]


def split_kernel(side_ref, dist_ref, far_ref, near_ref, rows_ref):
    side = side_ref[0]

    def step(v, carry):
        slot = v & 3
        rows_ref[slot] = dist_ref[v].astype(jnp.float32)
        far_ref[v] = rows_ref[slot, pl.ds(side, ROWS, stride=2), :].astype(jnp.bfloat16)
        near_ref[v] = rows_ref[slot, pl.ds(1 - side, ROWS, stride=2), :].astype(jnp.bfloat16)
        return carry

    lax.fori_loop(0, dist_ref.shape[0], step, 0, unroll=4)


def column_kernel(parts_ref, out_ref):
    for comp in range(5):
        total = parts_ref[0, comp].astype(jnp.float32)
        for part in range(1, parts_ref.shape[0]):
            total = total + parts_ref[part, comp].astype(jnp.float32)
        for copy in range(out_ref.shape[0]):
            out_ref[copy, comp] = total


def equilibrium(params, sx, sy, sz):
    dx, dy, dz = sx - params(0), sy - params(1), sz - params(2)
    spread = dx * dx + dy * dy + dz * dz
    return params(4) * jnp.exp2(spread * params(3))


def relax(value, params, sx, sy, sz):
    mixed = value * params(5) + equilibrium(params, sx, sy, sz)
    return mixed.astype(jnp.bfloat16).astype(jnp.float32)


def inner_kernel(
    side_ref, index_ref, sums_ref, dist_ref,
    moved_ref, table_ref, equil_ref, edge_params_ref, node_ref, own_ref,
):
    side = side_ref[0]
    fill_nodes(node_ref)
    for plane, part in [(plane, part) for plane in range(4) for part in range(2)]:
        core, first = plane // 2, 4 * (plane % 2) + 2 * part
        core = core + (1 - side) * (1 - 2 * core)
        total = [sums_ref[core, first, comp] + sums_ref[core, first + 1, comp] for comp in range(5)]
        density = total[0]
        inverse = 1.0 / density
        flow = [total[comp] * inverse for comp in (1, 2, 3)]
        speed2 = flow[0] * flow[0] + flow[1] * flow[1] + flow[2] * flow[2]
        temper = (total[4] * inverse + center - speed2) * (1.0 / 3.0)
        root = jnp.sqrt(temper)
        rate = (time_step * relax_coef) * density * root
        scale = density * ((2.0 * np.pi) ** -1.5) / (temper * root)
        keep = 1.0 / (1.0 + rate)
        values = flow + [(-0.5 * log2e) / temper, scale * (rate * keep), keep]
        for comp in range(6):
            if plane in (1, 2):
                own_ref[comp, pl.ds(2 * HALF * part + plane - 1, HALF, stride=2), :] = values[comp]
            else:
                edge_params_ref[plane // 3, comp, pl.ds(HALF * part, HALF), :] = values[comp]

    lane = lax.broadcasted_iota(jnp.int32, (8, LANES), 1)
    row = lax.broadcasted_iota(jnp.int32, (8, LANES), 0)
    column, upper, parity = lane & 63, lane >> 6, row & 1
    blocks = 2 * ROWS // 8

    def step(v, carry):
        sx, sy, sz = scalars(index_ref, node_ref, v)
        up_x, up_y, up_z = sx > 0.0, sy > 0.0, sz > 0.0
        ax, ay, az = (time_step * jnp.abs(s) for s in (sx, sy, sz))
        rest = 1.0 - (ax + ay + az)
        which = jnp.where(up_x, 0, 1)
        halo_x = parity == which
        table_ref[pl.ds(v, 1), :] = jnp.full((1, LANES), jnp.where(which == side, ax, -ax), jnp.float32)
        equil_ref[v] = equilibrium(lambda c: edge_params_ref[which, c], sx, sy, sz)
        shift_x = jnp.where(up_x, 1, 7)
        shift_y = jnp.where(up_y, 2, 6)
        last_y = (row >> 1) == jnp.where(up_y, 0, 3)
        wrap_y = upper == jnp.where(up_y, 0, 1)
        wrap_z = column == jnp.where(up_z, 0, 63)
        shift_z = jnp.where(up_z, 1, LANES - 1)
        values = []
        for k in range(blocks):
            rows = slice(8 * k, 8 * k + 8)
            raw = dist_ref[v, 16 * (k // 2):16 * (k // 2) + 16, :].astype(jnp.float32)
            part = raw[8 * (k % 2):8 * (k % 2) + 8]
            values.append(relax(part, lambda c: own_ref[c, rows, :], sx, sy, sz))
        swapped = [pltpu.roll(value, 64, 1) for value in values]
        turned = [pltpu.roll(value, shift_y, 0) for value in swapped]
        for k in range(blocks):
            value = values[k]
            from_x = jnp.where(halo_x, 0.0, pltpu.roll(value, shift_x, 0))
            beyond = jnp.where(up_y, turned[(k - 1) % blocks], turned[(k + 1) % blocks])
            from_y = jnp.where(wrap_y, jnp.where(last_y, beyond, turned[k]), swapped[k])
            near = pltpu.roll(value, shift_z, 1)
            from_z = jnp.where(wrap_z, pltpu.roll(near, 64, 1), near)
            moved_ref[v, 8 * k:8 * k + 8, :] = rest * value + ax * from_x + ay * from_y + az * from_z
        return carry

    lax.fori_loop(0, dist_ref.shape[0], step, 0, unroll=8)


def edge_kernel(
    side_ref, table_ref, equil_ref, edge_params_ref, across_ref, within_ref, moved_ref, out_hbm,
    out_ref, edge_ref, sems,
):
    side = side_ref[0]
    keep_across = edge_params_ref[side, 5]
    keep_within = edge_params_ref[1 - side, 5]
    far_rows = (lax.broadcasted_iota(jnp.int32, BOTH, 0) & 1) == side
    copies = sems.shape[0]
    count = across_ref.shape[0] // copies

    def step(v, slot):
        size = table_ref[pl.ds(v, 1), :]
        far = size > 0.0
        value = jnp.where(far, across_ref[v].astype(jnp.float32), within_ref[v].astype(jnp.float32))
        mixed = value * jnp.where(far, keep_across, keep_within) + equil_ref[v]
        edge = mixed.astype(jnp.bfloat16).astype(jnp.float32) * jnp.abs(size)
        edge_ref[slot, pl.ds(0, ROWS, stride=2), :] = edge
        edge_ref[slot, pl.ds(1, ROWS, stride=2), :] = edge
        added = jnp.where(far == far_rows, edge_ref[slot], 0.0)
        out_ref[v] = (moved_ref[v] + added).astype(jnp.bfloat16)

    def chunk(c, carry):
        for u in range(count):
            step(c * count + u, u)
        where = pl.ds(c * count, count)
        pltpu.make_async_copy(out_ref.at[where], out_hbm.at[where], sems.at[c]).start()
        return carry

    lax.fori_loop(0, copies, chunk, 0)
    for c in range(copies):
        where = pl.ds(c * count, count)
        pltpu.make_async_copy(out_ref.at[where], out_hbm.at[where], sems.at[c]).wait()


def shards(dist, vel_index, weight_int):
    count_v = dist.shape[0]
    side = lax.axis_index("xl")
    core = lax.axis_index("core")
    plane = jnp.reshape(1 ^ side ^ core, (1,)).astype(jnp.int32)
    side = jnp.reshape(side, (1,)).astype(jnp.int32)
    f32, bf16 = jnp.float32, jnp.bfloat16
    mixed = dist.reshape(count_v, 2, ROWS, LANES).transpose(0, 2, 1, 3).reshape((count_v,) + BOTH)

    partial_sums = pl.pallas_call(
        moments_kernel,
        out_shape=jax.ShapeDtypeStruct((2, 5) + CELLS, f32),
        in_specs=[HBM, HBM, HBM],
        out_specs=VMEM,
        scratch_shapes=[
            pltpu.SMEM(vel_index.shape, jnp.int32),
            pltpu.SMEM(weight_int.shape, jnp.int32),
            pltpu.SMEM((NODES,), f32),
            pltpu.VMEM(mixed.shape, bf16),
            pltpu.VMEM((5,) + BOTH, f32),
            pltpu.SemaphoreType.DMA((2,)),
            pltpu.SemaphoreType.DMA((4,)),
        ],
        compiler_params=small(56),
        name="moments",
    )(vel_index, weight_int, mixed)
    both = lax.all_gather(partial_sums, "core")
    chip = pl.pallas_call(
        chip_kernel,
        out_shape=jax.ShapeDtypeStruct((SIZES[2], 5, HALF, LANES), bf16),
        in_specs=[SMEM, VMEM],
        out_specs=VMEM,
        compiler_params=small(4),
        name="chip_sum",
    )(plane, both)
    parts = lax.all_to_all(chip, "y", 0, 0)

    count = SIZES[0] * SIZES[1]
    swap = [(i, i ^ 1) for i in range(count)]
    along = [(i, (i + 2 - 4 * (i % 2)) % count) for i in range(count)]
    half = jax.ShapeDtypeStruct((count_v,) + CELLS, bf16)
    far, near = pl.pallas_call(
        split_kernel,
        out_shape=(half, half),
        in_specs=[SMEM, VMEM],
        out_specs=(VMEM, VMEM),
        scratch_shapes=[pltpu.VMEM((4,) + BOTH, f32)],
        compiler_params=small(8),
        cost_estimate=pl.CostEstimate(flops=1 << 20, bytes_accessed=1 << 20, transcendentals=0),
        name="split_planes",
    )(side, mixed)

    def hand_on(planes, cost):
        return pl.pallas_call(
            copy_kernel,
            out_shape=half,
            in_specs=[VMEM],
            out_specs=VMEM,
            compiler_params=small(8),
            cost_estimate=pl.CostEstimate(flops=cost, bytes_accessed=1 << 19, transcendentals=0),
            name="hand_on",
        )(planes)

    across = lax.ppermute(hand_on(lax.ppermute(far, GX, swap), 1 << 31), GX, along)
    within = hand_on(lax.ppermute(near, GX, swap), 1 << 32)

    column = pl.pallas_call(
        column_kernel,
        out_shape=jax.ShapeDtypeStruct((8, 5, HALF, LANES), f32),
        in_specs=[VMEM],
        out_specs=VMEM,
        compiler_params=small(4),
        name="column_sum",
    )(parts)
    gathered = lax.all_to_all(column, NAMES, 0, 0, axis_index_groups=GROUPS)
    sums = lax.all_gather(gathered, "core")
    moved, table, equil, edge_params = pl.pallas_call(
        inner_kernel,
        out_shape=(
            jax.ShapeDtypeStruct(mixed.shape, f32),
            jax.ShapeDtypeStruct((count_v, LANES), f32),
            jax.ShapeDtypeStruct((count_v,) + CELLS, f32),
            jax.ShapeDtypeStruct((2, 6) + CELLS, f32),
        ),
        in_specs=[SMEM, SMEM, VMEM, VMEM],
        out_specs=(VMEM, VMEM, VMEM, VMEM),
        scratch_shapes=[pltpu.SMEM((NODES,), f32), pltpu.VMEM((6,) + BOTH, f32)],
        compiler_params=small(8),
        cost_estimate=pl.CostEstimate(flops=1, bytes_accessed=1, transcendentals=0),
        name="inner",
    )(side, vel_index, sums, mixed)
    out = pl.pallas_call(
        edge_kernel,
        out_shape=jax.ShapeDtypeStruct(mixed.shape, bf16),
        in_specs=[SMEM, VMEM, VMEM, VMEM, VMEM, VMEM, VMEM],
        out_specs=HBM,
        scratch_shapes=[
            pltpu.VMEM(mixed.shape, bf16),
            pltpu.VMEM((8,) + BOTH, f32),
            pltpu.SemaphoreType.DMA((4,)),
        ],
        compiler_params=small(8),
        name="edge",
    )(side, table, equil, edge_params, across, within, moved)
    return out.reshape(count_v, ROWS, 2, LANES).transpose(0, 2, 1, 3).reshape(dist.shape)


def solution(mesh):
    parts = Mesh(mesh.devices.reshape(SIZES), NAMES)
    return jax.shard_map(
        shards,
        mesh=parts,
        in_specs=(P(VERT, GX, None), P(None, VERT), P(VERT)),
        out_specs=P(VERT, GX, None),
        check_vma=False,
    )
```

```python
import jax
import jax.numpy as jnp
import numpy as np
from jax import lax
from jax.experimental import pallas as pl
from jax.experimental.pallas import tpu as pltpu
from jax.sharding import Mesh, PartitionSpec as P

NV = 1024
NODES = 33
ROWS = 32
LANES = 128
CELLS = (ROWS, LANES)
BOTH = (2 * ROWS, LANES)

speed_max = 4.0
time_step = 1.0 / 12.0
relax_coef = 0.1
center = 24.0
log2e = 1.4426950408889634

SIZES = (8, 2, 8, 2, 2)
NAMES = ("z", "xl", "y", "xh", "core")
GX = ("z", "xl")
VERT = ("y", "xh", "core")

VMEM = pl.BlockSpec(memory_space=pltpu.VMEM)
ANY = pl.BlockSpec(memory_space=pl.ANY)
HBM = pl.BlockSpec(memory_space=pltpu.HBM)
SMEM = pl.BlockSpec(memory_space=pltpu.SMEM)


HALF = ROWS // 2


def place(z, xl, y, xh, core):
    return ((((z % SIZES[0]) * 2 + xl) * SIZES[2] + y) * 2 + xh) * 2 + core


PAIRS = [[(z, 0, 0), (z, 1, 0)] for z in range(SIZES[0])] + [
    [(z, 1, 1), (z + 1, 0, 1)] for z in range(SIZES[0])
]
GROUPS = [
    [place(z, xl, y + odd, xh, core) for z, xl, core in pair for odd in range(2) for xh in range(2)]
    for pair in PAIRS
    for y in range(0, SIZES[2], 2)
]
NODE_SPEEDS = [float(speed_max * np.cos(np.pi * j / (NODES - 1))) for j in range(NODES)]


def fill_nodes(node_ref):
    for j, speed in enumerate(NODE_SPEEDS):
        node_ref[j] = jnp.float32(speed)


def scalars(index_ref, node_ref, v):
    return [node_ref[index_ref[comp, v]] for comp in range(3)]


def small(mebibytes):
    return pltpu.CompilerParams(vmem_limit_bytes=mebibytes << 20)


def moments_kernel(
    index_hbm, weight_hbm, dist_hbm, out_ref,
    index_ref, weight_ref, node_ref, dist_ref, sums_ref, table_sems, sems,
):
    count = dist_ref.shape[0]
    half = count // 2
    pieces = []
    for part in range(2):
        for k in range(2):
            where = (pl.ds(k * half, half), pl.ds(part * ROWS, ROWS))
            pieces.append(pltpu.make_async_copy(dist_hbm.at[where], dist_ref.at[where], sems.at[2 * part + k]))
    tables = [
        pltpu.make_async_copy(index_hbm, index_ref, table_sems.at[0]),
        pltpu.make_async_copy(weight_hbm, weight_ref, table_sems.at[1]),
    ]
    for copy in tables + pieces:
        copy.start()
    fill_nodes(node_ref)
    for copy in tables:
        copy.wait()
    for part in range(2):
        rows = pl.ds(part * ROWS, ROWS)
        sums = [jnp.zeros(CELLS, jnp.float32) for _ in range(5)]
        for v in range(count):
            if v % half == 0:
                pieces[2 * part + v // half].wait()
            sx, sy, sz = scalars(index_ref, node_ref, v)
            weight = weight_ref[v].astype(jnp.float32) * (512.0 / (32768.0 * NV))
            square = sx * sx + sy * sy + sz * sz - center
            value = weight * dist_ref[v, rows, :].astype(jnp.float32)
            terms = (value, sx * value, sy * value, sz * value, square * value)
            sums = [total + term for total, term in zip(sums, terms)]
        for comp in range(5):
            sums_ref[comp, rows, :] = sums[comp]
    for plane in range(2):
        for comp in range(5):
            out_ref[plane, comp] = sums_ref[comp, pl.ds(plane, ROWS, stride=2), :]


def chip_kernel(plane_ref, both_ref, out_ref):
    plane = plane_ref[0]
    for comp in range(5):
        total = (both_ref[0, plane, comp] + both_ref[1, plane, comp]).astype(out_ref.dtype)
        for y in range(out_ref.shape[0]):
            first = HALF * (y % 2)
            out_ref[y, comp] = total[first:first + HALF]


def far_kernel(side_ref, dist_ref, far_ref, rows_ref):
    side = side_ref[0]

    def step(v, carry):
        slot = v & 3
        rows_ref[slot] = dist_ref[v].astype(jnp.float32)
        far_ref[v] = rows_ref[slot, pl.ds(side, ROWS, stride=2), :].astype(jnp.bfloat16)
        return carry

    lax.fori_loop(0, dist_ref.shape[0], step, 0, unroll=4)


def merge_kernel(side_ref, index_ref, dist_ref, passed_ref, sent_ref, node_ref, rows_ref):
    side = side_ref[0]
    fill_nodes(node_ref)

    def step(v, carry):
        slot = v & 3
        up = jnp.where(node_ref[index_ref[0, v]] > 0.0, 1, 0)
        rows_ref[slot] = dist_ref[v].astype(jnp.float32)
        own = rows_ref[slot, pl.ds(1 - side, ROWS, stride=2), :].astype(jnp.bfloat16)
        sent_ref[v] = jnp.where(up == side, passed_ref[v], own)
        return carry

    lax.fori_loop(0, dist_ref.shape[0], step, 0, unroll=4)


def column_kernel(parts_ref, out_ref):
    for comp in range(5):
        total = parts_ref[0, comp].astype(jnp.float32)
        for part in range(1, parts_ref.shape[0]):
            total = total + parts_ref[part, comp].astype(jnp.float32)
        for copy in range(out_ref.shape[0]):
            out_ref[copy, comp] = total


def equilibrium(params, sx, sy, sz):
    dx, dy, dz = sx - params(0), sy - params(1), sz - params(2)
    spread = dx * dx + dy * dy + dz * dz
    return params(4) * jnp.exp2(spread * params(3))


def relax(value, params, sx, sy, sz):
    mixed = value * params(5) + equilibrium(params, sx, sy, sz)
    return mixed.astype(jnp.bfloat16).astype(jnp.float32)


def inner_kernel(
    side_ref, index_any, sums_ref, dist_ref,
    moved_ref, table_ref, equil_ref, edge_params_ref, index_ref, node_ref, own_ref, sem,
):
    side = side_ref[0]
    indices = pltpu.make_async_copy(index_any, index_ref, sem.at[0])
    indices.start()
    fill_nodes(node_ref)
    for plane, part in [(plane, part) for plane in range(4) for part in range(2)]:
        core, first = plane // 2, 4 * (plane % 2) + 2 * part
        core = core + (1 - side) * (1 - 2 * core)
        total = [sums_ref[core, first, comp] + sums_ref[core, first + 1, comp] for comp in range(5)]
        density = total[0]
        inverse = 1.0 / density
        flow = [total[comp] * inverse for comp in (1, 2, 3)]
        speed2 = flow[0] * flow[0] + flow[1] * flow[1] + flow[2] * flow[2]
        temper = (total[4] * inverse + center - speed2) * (1.0 / 3.0)
        root = jnp.sqrt(temper)
        rate = (time_step * relax_coef) * density * root
        scale = density * ((2.0 * np.pi) ** -1.5) / (temper * root)
        keep = 1.0 / (1.0 + rate)
        values = flow + [(-0.5 * log2e) / temper, scale * (rate * keep), keep]
        for comp in range(6):
            if plane in (1, 2):
                own_ref[comp, pl.ds(2 * HALF * part + plane - 1, HALF, stride=2), :] = values[comp]
            else:
                edge_params_ref[plane // 3, comp, pl.ds(HALF * part, HALF), :] = values[comp]

    indices.wait()
    lane = lax.broadcasted_iota(jnp.int32, (8, LANES), 1)
    row = lax.broadcasted_iota(jnp.int32, (8, LANES), 0)
    column, upper, parity = lane & 63, lane >> 6, row & 1
    blocks = 2 * ROWS // 8

    def step(v, carry):
        sx, sy, sz = scalars(index_ref, node_ref, v)
        up_x, up_y, up_z = sx > 0.0, sy > 0.0, sz > 0.0
        ax, ay, az = (time_step * jnp.abs(s) for s in (sx, sy, sz))
        rest = 1.0 - (ax + ay + az)
        which = jnp.where(up_x, 0, 1)
        halo_x = parity == which
        table_ref[pl.ds(v, 1), :] = jnp.full((1, LANES), jnp.where(which == side, ax, -ax), jnp.float32)
        equil_ref[v] = equilibrium(lambda c: edge_params_ref[which, c], sx, sy, sz)
        shift_x = jnp.where(up_x, 1, 7)
        shift_y = jnp.where(up_y, 2, 6)
        last_y = (row >> 1) == jnp.where(up_y, 0, 3)
        wrap_y = upper == jnp.where(up_y, 0, 1)
        wrap_z = column == jnp.where(up_z, 0, 63)
        shift_z = jnp.where(up_z, 1, LANES - 1)
        values = []
        for k in range(blocks):
            rows = slice(8 * k, 8 * k + 8)
            raw = dist_ref[v, 16 * (k // 2):16 * (k // 2) + 16, :].astype(jnp.float32)
            part = raw[8 * (k % 2):8 * (k % 2) + 8]
            values.append(relax(part, lambda c: own_ref[c, rows, :], sx, sy, sz))
        swapped = [pltpu.roll(value, 64, 1) for value in values]
        turned = [pltpu.roll(value, shift_y, 0) for value in swapped]
        for k in range(blocks):
            value = values[k]
            from_x = jnp.where(halo_x, 0.0, pltpu.roll(value, shift_x, 0))
            beyond = jnp.where(up_y, turned[(k - 1) % blocks], turned[(k + 1) % blocks])
            from_y = jnp.where(wrap_y, jnp.where(last_y, beyond, turned[k]), swapped[k])
            near = pltpu.roll(value, shift_z, 1)
            from_z = jnp.where(wrap_z, pltpu.roll(near, 64, 1), near)
            moved_ref[v, 8 * k:8 * k + 8, :] = rest * value + ax * from_x + ay * from_y + az * from_z
        return carry

    lax.fori_loop(0, dist_ref.shape[0], step, 0, unroll=8)


def edge_kernel(
    side_ref, table_ref, equil_ref, edge_params_ref, halo_ref, moved_ref, out_hbm,
    out_ref, edge_ref, sems,
):
    side = side_ref[0]
    keep_across = edge_params_ref[side, 5]
    keep_within = edge_params_ref[1 - side, 5]
    far_rows = (lax.broadcasted_iota(jnp.int32, BOTH, 0) & 1) == side
    copies = sems.shape[0]
    count = halo_ref.shape[0] // copies

    def step(v, slot):
        size = table_ref[pl.ds(v, 1), :]
        far = size > 0.0
        value = halo_ref[v].astype(jnp.float32)
        mixed = value * jnp.where(far, keep_across, keep_within) + equil_ref[v]
        edge = mixed.astype(jnp.bfloat16).astype(jnp.float32) * jnp.abs(size)
        edge_ref[slot, pl.ds(0, ROWS, stride=2), :] = edge
        edge_ref[slot, pl.ds(1, ROWS, stride=2), :] = edge
        added = jnp.where(far == far_rows, edge_ref[slot], 0.0)
        out_ref[v] = (moved_ref[v] + added).astype(jnp.bfloat16)

    def chunk(c, carry):
        for u in range(count):
            step(c * count + u, u)
        where = pl.ds(c * count, count)
        pltpu.make_async_copy(out_ref.at[where], out_hbm.at[where], sems.at[c]).start()
        return carry

    lax.fori_loop(0, copies, chunk, 0)
    for c in range(copies):
        where = pl.ds(c * count, count)
        pltpu.make_async_copy(out_ref.at[where], out_hbm.at[where], sems.at[c]).wait()


def shards(dist, vel_index, weight_int):
    count_v = dist.shape[0]
    side = lax.axis_index("xl")
    core = lax.axis_index("core")
    plane = jnp.reshape(1 ^ side ^ core, (1,)).astype(jnp.int32)
    side = jnp.reshape(side, (1,)).astype(jnp.int32)
    f32, bf16 = jnp.float32, jnp.bfloat16
    mixed = dist.reshape(count_v, 2, ROWS, LANES).transpose(0, 2, 1, 3).reshape((count_v,) + BOTH)

    partial_sums = pl.pallas_call(
        moments_kernel,
        out_shape=jax.ShapeDtypeStruct((2, 5) + CELLS, f32),
        in_specs=[HBM, HBM, HBM],
        out_specs=VMEM,
        scratch_shapes=[
            pltpu.SMEM(vel_index.shape, jnp.int32),
            pltpu.SMEM(weight_int.shape, jnp.int32),
            pltpu.SMEM((NODES,), f32),
            pltpu.VMEM(mixed.shape, bf16),
            pltpu.VMEM((5,) + BOTH, f32),
            pltpu.SemaphoreType.DMA((2,)),
            pltpu.SemaphoreType.DMA((4,)),
        ],
        compiler_params=small(56),
        name="moments",
    )(vel_index, weight_int, mixed)
    both = lax.all_gather(partial_sums, "core")
    chip = pl.pallas_call(
        chip_kernel,
        out_shape=jax.ShapeDtypeStruct((SIZES[2], 5, HALF, LANES), bf16),
        in_specs=[SMEM, VMEM],
        out_specs=VMEM,
        compiler_params=small(4),
        name="chip_sum",
    )(plane, both)
    parts = lax.all_to_all(chip, "y", 0, 0)

    count = SIZES[0] * SIZES[1]
    swap = [(i, i ^ 1) for i in range(count)]
    along = [(i, (i - 2 + 4 * (i % 2)) % count) for i in range(count)]
    half = jax.ShapeDtypeStruct((count_v,) + CELLS, bf16)
    far = pl.pallas_call(
        far_kernel,
        out_shape=half,
        in_specs=[SMEM, VMEM],
        out_specs=VMEM,
        scratch_shapes=[pltpu.VMEM((4,) + BOTH, f32)],
        compiler_params=small(8),
        cost_estimate=pl.CostEstimate(flops=1 << 20, bytes_accessed=1 << 20, transcendentals=0),
        name="far_planes",
    )(side, mixed)
    passed = lax.ppermute(far, GX, along)
    sent = pl.pallas_call(
        merge_kernel,
        out_shape=half,
        in_specs=[SMEM, SMEM, VMEM, VMEM],
        out_specs=VMEM,
        scratch_shapes=[pltpu.SMEM((NODES,), f32), pltpu.VMEM((4,) + BOTH, f32)],
        compiler_params=small(8),
        cost_estimate=pl.CostEstimate(flops=1 << 32, bytes_accessed=1 << 20, transcendentals=0),
        name="upwind_planes",
    )(side, vel_index, mixed, passed)
    halo = lax.ppermute(sent, GX, swap)

    column = pl.pallas_call(
        column_kernel,
        out_shape=jax.ShapeDtypeStruct((8, 5, HALF, LANES), f32),
        in_specs=[VMEM],
        out_specs=VMEM,
        compiler_params=small(4),
        name="column_sum",
    )(parts)
    gathered = lax.all_to_all(column, NAMES, 0, 0, axis_index_groups=GROUPS)
    sums = lax.all_gather(gathered, "core")
    moved, table, equil, edge_params = pl.pallas_call(
        inner_kernel,
        out_shape=(
            jax.ShapeDtypeStruct(mixed.shape, f32),
            jax.ShapeDtypeStruct((count_v, LANES), f32),
            jax.ShapeDtypeStruct((count_v,) + CELLS, f32),
            jax.ShapeDtypeStruct((2, 6) + CELLS, f32),
        ),
        in_specs=[SMEM, ANY, VMEM, VMEM],
        out_specs=(VMEM, VMEM, VMEM, VMEM),
        scratch_shapes=[
            pltpu.SMEM(vel_index.shape, jnp.int32),
            pltpu.SMEM((NODES,), f32),
            pltpu.VMEM((6,) + BOTH, f32),
            pltpu.SemaphoreType.DMA((1,)),
        ],
        compiler_params=small(8),
        cost_estimate=pl.CostEstimate(flops=1, bytes_accessed=1, transcendentals=0),
        name="inner",
    )(side, vel_index, sums, mixed)
    out = pl.pallas_call(
        edge_kernel,
        out_shape=jax.ShapeDtypeStruct(mixed.shape, bf16),
        in_specs=[SMEM, VMEM, VMEM, VMEM, VMEM, VMEM],
        out_specs=HBM,
        scratch_shapes=[
            pltpu.VMEM(mixed.shape, bf16),
            pltpu.VMEM((8,) + BOTH, f32),
            pltpu.SemaphoreType.DMA((4,)),
        ],
        compiler_params=small(8),
        name="edge",
    )(side, table, equil, edge_params, halo, moved)
    return out.reshape(count_v, ROWS, 2, LANES).transpose(0, 2, 1, 3).reshape(dist.shape)


def solution(mesh):
    parts = Mesh(mesh.devices.reshape(SIZES), NAMES)
    return jax.shard_map(
        shards,
        mesh=parts,
        in_specs=(P(VERT, GX, None), P(None, VERT), P(VERT)),
        out_specs=P(VERT, GX, None),
        check_vma=False,
    )
```

```python
import jax
import jax.numpy as jnp
import numpy as np
from jax import lax
from jax.experimental import pallas as pl
from jax.experimental.pallas import tpu as pltpu
from jax.sharding import Mesh, PartitionSpec as P

NV = 1024
NODES = 33
ROWS = 32
LANES = 128
CELLS = (ROWS, LANES)
BOTH = (2 * ROWS, LANES)

speed_max = 4.0
time_step = 1.0 / 12.0
relax_coef = 0.1
center = 24.0
log2e = 1.4426950408889634

SIZES = (8, 2, 8, 2, 2)
NAMES = ("z", "xl", "y", "xh", "core")
GX = ("z", "xl")
VERT = ("y", "xh", "core")

VMEM = pl.BlockSpec(memory_space=pltpu.VMEM)
ANY = pl.BlockSpec(memory_space=pl.ANY)
HBM = pl.BlockSpec(memory_space=pltpu.HBM)
SMEM = pl.BlockSpec(memory_space=pltpu.SMEM)


HALF = ROWS // 2


def place(z, xl, y, xh, core):
    return ((((z % SIZES[0]) * 2 + xl) * SIZES[2] + y) * 2 + xh) * 2 + core


PAIRS = [[(z, 0, 0), (z, 1, 0)] for z in range(SIZES[0])] + [
    [(z, 1, 1), (z + 1, 0, 1)] for z in range(SIZES[0])
]
GROUPS = [
    [place(z, xl, y + odd, xh, core) for z, xl, core in pair for odd in range(2) for xh in range(2)]
    for pair in PAIRS
    for y in range(0, SIZES[2], 2)
]
MOMENTS_VMEM = 56254464
NODE_SPEEDS = [float(speed_max * np.cos(np.pi * j / (NODES - 1))) for j in range(NODES)]


def fill_nodes(node_ref):
    for j, speed in enumerate(NODE_SPEEDS):
        node_ref[j] = jnp.float32(speed)


def scalars(index_ref, node_ref, v):
    return [node_ref[index_ref[comp, v]] for comp in range(3)]


def small(mebibytes):
    return pltpu.CompilerParams(vmem_limit_bytes=mebibytes << 20)


def moments_kernel(
    index_hbm, weight_hbm, dist_hbm, out_ref,
    index_ref, weight_ref, node_ref, dist_ref, sums_ref, table_sems, sems,
):
    count = dist_ref.shape[0]
    half = count // 2
    pieces = []
    for part in range(2):
        for k in range(2):
            where = (pl.ds(k * half, half), pl.ds(part * ROWS, ROWS))
            pieces.append(pltpu.make_async_copy(dist_hbm.at[where], dist_ref.at[where], sems.at[2 * part + k]))
    tables = [
        pltpu.make_async_copy(index_hbm, index_ref, table_sems.at[0]),
        pltpu.make_async_copy(weight_hbm, weight_ref, table_sems.at[1]),
    ]
    for copy in tables + pieces:
        copy.start()
    fill_nodes(node_ref)
    for copy in tables:
        copy.wait()
    for part in range(2):
        rows = pl.ds(part * ROWS, ROWS)
        sums = [jnp.zeros(CELLS, jnp.float32) for _ in range(5)]
        for v in range(count):
            if v % half == 0:
                pieces[2 * part + v // half].wait()
            sx, sy, sz = scalars(index_ref, node_ref, v)
            weight = weight_ref[v].astype(jnp.float32) * (512.0 / (32768.0 * NV))
            square = sx * sx + sy * sy + sz * sz - center
            value = weight * dist_ref[v, rows, :].astype(jnp.float32)
            terms = (value, sx * value, sy * value, sz * value, square * value)
            sums = [total + term for total, term in zip(sums, terms)]
        for comp in range(5):
            sums_ref[comp, rows, :] = sums[comp]
    for plane in range(2):
        for comp in range(5):
            out_ref[plane, comp] = sums_ref[comp, pl.ds(plane, ROWS, stride=2), :]


def chip_kernel(plane_ref, both_ref, out_ref):
    plane = plane_ref[0]
    for comp in range(5):
        total = (both_ref[0, plane, comp] + both_ref[1, plane, comp]).astype(out_ref.dtype)
        for y in range(out_ref.shape[0]):
            first = HALF * (y % 2)
            out_ref[y, comp] = total[first:first + HALF]


def far_kernel(side_ref, dist_ref, far_ref, rows_ref):
    side = side_ref[0]

    def step(v, carry):
        slot = v & 3
        rows_ref[slot] = dist_ref[v].astype(jnp.float32)
        far_ref[v] = rows_ref[slot, pl.ds(side, ROWS, stride=2), :].astype(jnp.bfloat16)
        return carry

    lax.fori_loop(0, dist_ref.shape[0], step, 0, unroll=4)


def merge_kernel(side_ref, index_ref, dist_ref, passed_ref, sent_ref, node_ref, rows_ref):
    side = side_ref[0]
    fill_nodes(node_ref)

    def step(v, carry):
        slot = v & 3
        up = jnp.where(node_ref[index_ref[0, v]] > 0.0, 1, 0)
        rows_ref[slot] = dist_ref[v].astype(jnp.float32)
        own = rows_ref[slot, pl.ds(1 - side, ROWS, stride=2), :].astype(jnp.bfloat16)
        sent_ref[v] = jnp.where(up == side, passed_ref[v], own)
        return carry

    lax.fori_loop(0, dist_ref.shape[0], step, 0, unroll=4)


def column_kernel(parts_ref, out_ref):
    for comp in range(5):
        total = parts_ref[0, comp].astype(jnp.float32)
        for part in range(1, parts_ref.shape[0]):
            total = total + parts_ref[part, comp].astype(jnp.float32)
        for copy in range(out_ref.shape[0]):
            out_ref[copy, comp] = total


def equilibrium(params, sx, sy, sz):
    dx, dy, dz = sx - params(0), sy - params(1), sz - params(2)
    spread = dx * dx + dy * dy + dz * dz
    return params(4) * jnp.exp2(spread * params(3))


def relax(value, params, sx, sy, sz):
    mixed = value * params(5) + equilibrium(params, sx, sy, sz)
    return mixed.astype(jnp.bfloat16).astype(jnp.float32)


def inner_kernel(
    side_ref, index_any, sums_ref, dist_ref,
    moved_ref, table_ref, equil_ref, edge_params_ref, index_ref, node_ref, own_ref, sem,
):
    side = side_ref[0]
    indices = pltpu.make_async_copy(index_any, index_ref, sem.at[0])
    indices.start()
    fill_nodes(node_ref)
    for plane, part in [(plane, part) for plane in range(4) for part in range(2)]:
        core, first = plane // 2, 4 * (plane % 2) + 2 * part
        core = core + (1 - side) * (1 - 2 * core)
        total = [sums_ref[core, first, comp] + sums_ref[core, first + 1, comp] for comp in range(5)]
        density = total[0]
        inverse = 1.0 / density
        flow = [total[comp] * inverse for comp in (1, 2, 3)]
        speed2 = flow[0] * flow[0] + flow[1] * flow[1] + flow[2] * flow[2]
        temper = (total[4] * inverse + center - speed2) * (1.0 / 3.0)
        root = jnp.sqrt(temper)
        rate = (time_step * relax_coef) * density * root
        scale = density * ((2.0 * np.pi) ** -1.5) / (temper * root)
        keep = 1.0 / (1.0 + rate)
        values = flow + [(-0.5 * log2e) / temper, scale * (rate * keep), keep]
        for comp in range(6):
            if plane in (1, 2):
                own_ref[comp, pl.ds(2 * HALF * part + plane - 1, HALF, stride=2), :] = values[comp]
            else:
                edge_params_ref[plane // 3, comp, pl.ds(HALF * part, HALF), :] = values[comp]

    indices.wait()
    lane = lax.broadcasted_iota(jnp.int32, (8, LANES), 1)
    row = lax.broadcasted_iota(jnp.int32, (8, LANES), 0)
    column, upper, parity = lane & 63, lane >> 6, row & 1
    blocks = 2 * ROWS // 8

    def step(v, carry):
        sx, sy, sz = scalars(index_ref, node_ref, v)
        up_x, up_y, up_z = sx > 0.0, sy > 0.0, sz > 0.0
        ax, ay, az = (time_step * jnp.abs(s) for s in (sx, sy, sz))
        rest = 1.0 - (ax + ay + az)
        which = jnp.where(up_x, 0, 1)
        halo_x = parity == which
        table_ref[pl.ds(v, 1), :] = jnp.full((1, LANES), jnp.where(which == side, ax, -ax), jnp.float32)
        equil_ref[v] = equilibrium(lambda c: edge_params_ref[which, c], sx, sy, sz)
        shift_x = jnp.where(up_x, 1, 7)
        shift_y = jnp.where(up_y, 2, 6)
        last_y = (row >> 1) == jnp.where(up_y, 0, 3)
        wrap_y = upper == jnp.where(up_y, 0, 1)
        wrap_z = column == jnp.where(up_z, 0, 63)
        shift_z = jnp.where(up_z, 1, LANES - 1)
        values = []
        for k in range(blocks):
            rows = slice(8 * k, 8 * k + 8)
            raw = dist_ref[v, 16 * (k // 2):16 * (k // 2) + 16, :].astype(jnp.float32)
            part = raw[8 * (k % 2):8 * (k % 2) + 8]
            values.append(relax(part, lambda c: own_ref[c, rows, :], sx, sy, sz))
        swapped = [pltpu.roll(value, 64, 1) for value in values]
        turned = [pltpu.roll(value, shift_y, 0) for value in swapped]
        for k in range(blocks):
            value = values[k]
            from_x = jnp.where(halo_x, 0.0, pltpu.roll(value, shift_x, 0))
            beyond = jnp.where(up_y, turned[(k - 1) % blocks], turned[(k + 1) % blocks])
            from_y = jnp.where(wrap_y, jnp.where(last_y, beyond, turned[k]), swapped[k])
            near = pltpu.roll(value, shift_z, 1)
            from_z = jnp.where(wrap_z, pltpu.roll(near, 64, 1), near)
            moved_ref[v, 8 * k:8 * k + 8, :] = rest * value + ax * from_x + ay * from_y + az * from_z
        return carry

    lax.fori_loop(0, dist_ref.shape[0], step, 0, unroll=8)


def edge_kernel(
    side_ref, table_ref, equil_ref, edge_params_ref, halo_ref, moved_ref, out_hbm,
    out_ref, edge_ref, sems,
):
    side = side_ref[0]
    keep_across = edge_params_ref[side, 5]
    keep_within = edge_params_ref[1 - side, 5]
    far_rows = (lax.broadcasted_iota(jnp.int32, BOTH, 0) & 1) == side
    copies = sems.shape[0]
    count = halo_ref.shape[0] // copies

    def step(v, slot):
        size = table_ref[pl.ds(v, 1), :]
        far = size > 0.0
        value = halo_ref[v].astype(jnp.float32)
        mixed = value * jnp.where(far, keep_across, keep_within) + equil_ref[v]
        edge = mixed.astype(jnp.bfloat16).astype(jnp.float32) * jnp.abs(size)
        edge_ref[slot, pl.ds(0, ROWS, stride=2), :] = edge
        edge_ref[slot, pl.ds(1, ROWS, stride=2), :] = edge
        added = jnp.where(far == far_rows, edge_ref[slot], 0.0)
        out_ref[v] = (moved_ref[v] + added).astype(jnp.bfloat16)

    def chunk(c, carry):
        for u in range(count):
            step(c * count + u, u)
        where = pl.ds(c * count, count)
        pltpu.make_async_copy(out_ref.at[where], out_hbm.at[where], sems.at[c]).start()
        return carry

    lax.fori_loop(0, copies, chunk, 0)
    for c in range(copies):
        where = pl.ds(c * count, count)
        pltpu.make_async_copy(out_ref.at[where], out_hbm.at[where], sems.at[c]).wait()


def shards(dist, vel_index, weight_int):
    count_v = dist.shape[0]
    side = lax.axis_index("xl")
    core = lax.axis_index("core")
    plane = jnp.reshape(1 ^ side ^ core, (1,)).astype(jnp.int32)
    side = jnp.reshape(side, (1,)).astype(jnp.int32)
    f32, bf16 = jnp.float32, jnp.bfloat16
    mixed = dist.reshape(count_v, 2, ROWS, LANES).transpose(0, 2, 1, 3).reshape((count_v,) + BOTH)

    partial_sums = pl.pallas_call(
        moments_kernel,
        out_shape=jax.ShapeDtypeStruct((2, 5) + CELLS, f32),
        in_specs=[HBM, HBM, HBM],
        out_specs=VMEM,
        scratch_shapes=[
            pltpu.SMEM(vel_index.shape, jnp.int32),
            pltpu.SMEM(weight_int.shape, jnp.int32),
            pltpu.SMEM((NODES,), f32),
            pltpu.VMEM(mixed.shape, bf16),
            pltpu.VMEM((5,) + BOTH, f32),
            pltpu.SemaphoreType.DMA((2,)),
            pltpu.SemaphoreType.DMA((4,)),
        ],
        compiler_params=pltpu.CompilerParams(vmem_limit_bytes=MOMENTS_VMEM),
        name="moments",
    )(vel_index, weight_int, mixed)
    both = lax.all_gather(partial_sums, "core")
    chip = pl.pallas_call(
        chip_kernel,
        out_shape=jax.ShapeDtypeStruct((SIZES[2], 5, HALF, LANES), bf16),
        in_specs=[SMEM, VMEM],
        out_specs=VMEM,
        compiler_params=small(4),
        name="chip_sum",
    )(plane, both)
    parts = lax.all_to_all(chip, "y", 0, 0)

    count = SIZES[0] * SIZES[1]
    swap = [(i, i ^ 1) for i in range(count)]
    along = [(i, (i - 2 + 4 * (i % 2)) % count) for i in range(count)]
    half = jax.ShapeDtypeStruct((count_v,) + CELLS, bf16)
    far = pl.pallas_call(
        far_kernel,
        out_shape=half,
        in_specs=[SMEM, VMEM],
        out_specs=VMEM,
        scratch_shapes=[pltpu.VMEM((4,) + BOTH, f32)],
        compiler_params=small(8),
        cost_estimate=pl.CostEstimate(flops=1 << 20, bytes_accessed=1 << 20, transcendentals=0),
        name="far_planes",
    )(side, mixed)
    passed = lax.ppermute(far, GX, along)
    sent = pl.pallas_call(
        merge_kernel,
        out_shape=half,
        in_specs=[SMEM, SMEM, VMEM, VMEM],
        out_specs=VMEM,
        scratch_shapes=[pltpu.SMEM((NODES,), f32), pltpu.VMEM((4,) + BOTH, f32)],
        compiler_params=small(8),
        cost_estimate=pl.CostEstimate(flops=1 << 32, bytes_accessed=1 << 20, transcendentals=0),
        name="upwind_planes",
    )(side, vel_index, mixed, passed)
    halo = lax.ppermute(sent, GX, swap)

    column = pl.pallas_call(
        column_kernel,
        out_shape=jax.ShapeDtypeStruct((8, 5, HALF, LANES), f32),
        in_specs=[VMEM],
        out_specs=VMEM,
        compiler_params=small(4),
        name="column_sum",
    )(parts)
    gathered = lax.all_to_all(column, NAMES, 0, 0, axis_index_groups=GROUPS)
    sums = lax.all_gather(gathered, "core")
    moved, table, equil, edge_params = pl.pallas_call(
        inner_kernel,
        out_shape=(
            jax.ShapeDtypeStruct(mixed.shape, f32),
            jax.ShapeDtypeStruct((count_v, LANES), f32),
            jax.ShapeDtypeStruct((count_v,) + CELLS, f32),
            jax.ShapeDtypeStruct((2, 6) + CELLS, f32),
        ),
        in_specs=[SMEM, ANY, VMEM, VMEM],
        out_specs=(VMEM, VMEM, VMEM, VMEM),
        scratch_shapes=[
            pltpu.SMEM(vel_index.shape, jnp.int32),
            pltpu.SMEM((NODES,), f32),
            pltpu.VMEM((6,) + BOTH, f32),
            pltpu.SemaphoreType.DMA((1,)),
        ],
        compiler_params=small(8),
        cost_estimate=pl.CostEstimate(flops=1, bytes_accessed=1, transcendentals=0),
        name="inner",
    )(side, vel_index, sums, mixed)
    out = pl.pallas_call(
        edge_kernel,
        out_shape=jax.ShapeDtypeStruct(mixed.shape, bf16),
        in_specs=[SMEM, VMEM, VMEM, VMEM, VMEM, VMEM],
        out_specs=HBM,
        scratch_shapes=[
            pltpu.VMEM(mixed.shape, bf16),
            pltpu.VMEM((8,) + BOTH, f32),
            pltpu.SemaphoreType.DMA((4,)),
        ],
        compiler_params=small(8),
        name="edge",
    )(side, table, equil, edge_params, halo, moved)
    return out.reshape(count_v, ROWS, 2, LANES).transpose(0, 2, 1, 3).reshape(dist.shape)


def solution(mesh):
    parts = Mesh(mesh.devices.reshape(SIZES), NAMES)
    return jax.shard_map(
        shards,
        mesh=parts,
        in_specs=(P(VERT, GX, None), P(None, VERT), P(VERT)),
        out_specs=P(VERT, GX, None),
        check_vma=False,
    )
```
